256 devices in a mesh: member: 8 (over z), band: 16 (over x_lo, y, core), tensor: 2 (over x_hi).
Axes of the slice: x: 4 (x_hi: 2, x_lo: 2; x = x_hi * 2 + x_lo), y: 4, z: 8, core: 2. Of those that a mesh axis runs over, the one named last changes fastest.
Arguments:
- prior_grids: bfloat16 [8, 4, 128, 128, 192], P('member', None, 'band'), may hold values from -6 to 6
- w_qkv: bfloat16 [192, 3, 192], P(None, None, 'tensor'), may hold values from -0.4375 to 0.4375
- w_out: bfloat16 [192, 192], P('tensor'), may hold values from -0.4375 to 0.4375
- w_up: bfloat16 [192, 768], P(None, 'tensor'), may hold values from -0.4375 to 0.4375
- w_down: bfloat16 [768, 192], P('tensor'), may hold values from -0.21875 to 0.21875
- head_weight: bfloat16 [192, 160], replicated, may hold values from -0.4375 to 0.4375
- pos_bias: bfloat16 [6, 128, 128], P('tensor'), may hold values from -6 to 400
- zonal_offsets: int32 [8], P('member'), may hold values from 0 to 127
- obs_index: int32 [2, 128, 128, 16], P('tensor', 'band', 'member'), may hold values from 0 to 319
- obs_count: int32 [2, 128, 128], P('tensor', 'band', 'member'), may hold values from 8 to 16
- obs_value: float32 [2, 128, 128, 16], P('tensor', 'band', 'member'), may hold values from -6 to 6
- obs_weight: float32 [2, 128, 128, 16], P('tensor', 'band', 'member'), may hold values from 1 to 30
Outputs:
- analysis: float32 [8, 4, 128, 128, 160], P(None, 'tensor', 'band', 'member')
The draws below stay inside these ranges and needn't reach their ends.
All inputs are finite; a program needn't handle non-finite values.
Results may differ from the reference program's by a relative error of at most 0.025.
Values may be sent and summed in bfloat16 or wider, within the bound.
A program may use at most 64 MiB of HBM per device.

```python
import math
import jax
import jax.numpy as jnp
from jax import lax

C = 192
HEADS = 6
FF = 768
PATCH_PREDICTED = 160
HEAD_DIM = 32
LEV = 4
LAT_DEV = 8
WLON = 8
VERTICAL_DEPTH = 2
WTOK = 128
ZONAL_CELLS = 128
NOBS = 16
NEWTON = 8
SAMPLE_COUNT = 8
MERIDIAN_CELLS = 128
LEVW = 2
NS = 320


def draw_pos_bias(key, part):
    key_base = jax.random.fold_in(key, 11)
    base = jnp.clip(jax.random.normal(key_base, (HEADS, WTOK, WTOK), jnp.float32), -6.0, 6.0)
    return base.astype(jnp.bfloat16)


def with_ends(values, stream_key, least, top_value):
    longest = values.shape.index(max(values.shape))
    spots = []
    for shift in (0, 1):
        where = [jax.random.randint(jax.random.fold_in(stream_key, axis), (), 0, length) for axis, length in enumerate(values.shape)]
        where[longest] = (where[longest] + shift) % values.shape[longest]
        spots.append(tuple(where))
    return values.at[spots[0]].set(least).at[spots[1]].set(top_value)


def levels(rng, extent, shards, least, top_value):
    loudness = 1.0
    for position, shards_of in shards:
        draws = jax.random.uniform(jax.random.fold_in(jax.random.fold_in(rng, 6), position), (shards_of,), jnp.float32, least / len(shards), top_value / len(shards))
        loudness = loudness * jnp.repeat(jnp.exp(draws), extent[position] // shards_of).reshape((-1,) + (1,) * (len(extent) - 1 - position))
    return loudness


def gaussian(key, shape, deviation, reach, cuts=(), kind=jnp.bfloat16):
    values = deviation * jax.random.normal(key, shape, jnp.float32)
    if cuts:
        values = values * levels(key, shape, cuts, -0.22, 0.18)
    return jnp.clip(values, -reach, reach).astype(kind)


def setup_inputs(seed: int = 0) -> dict:
    splits = jax.random.split(jax.random.key(seed), 13)
    return {
        "prior_grids": gaussian(splits[0], (SAMPLE_COUNT, LEV, MERIDIAN_CELLS, ZONAL_CELLS, C), 1.0, 6.0, ((0, 8), (2, 16))),
        "w_qkv": gaussian(splits[1], (C, 3, C), C ** -0.5, 0.4375, ((2, 2),)),
        "w_out": gaussian(splits[2], (C, C), C ** -0.5, 0.4375, ((0, 2),)),
        "w_up": gaussian(splits[3], (C, FF), C ** -0.5, 0.4375, ((1, 2),)),
        "w_down": gaussian(splits[4], (FF, C), FF ** -0.5, 0.21875, ((0, 2),)),
        "head_weight": gaussian(splits[5], (C, PATCH_PREDICTED), C ** -0.5, 0.4375),
        "pos_bias": draw_pos_bias(jax.random.fold_in(splits[12], 71), 0),
        "zonal_offsets": with_ends(jax.random.randint(splits[7], (SAMPLE_COUNT,), 0, ZONAL_CELLS), jax.random.fold_in(splits[7], 1), 0, ZONAL_CELLS - 1).astype(jnp.int32),
        "obs_index": with_ends(jax.random.randint(splits[8], (LEVW, MERIDIAN_CELLS, ZONAL_CELLS, NOBS), 0, NS), jax.random.fold_in(splits[8], 1), 0, NS - 1).astype(jnp.int32),
        "obs_count": with_ends(jax.random.randint(splits[9], (LEVW, MERIDIAN_CELLS, ZONAL_CELLS), NOBS // 2, NOBS + 1), jax.random.fold_in(splits[9], 1), NOBS // 2, NOBS).astype(jnp.int32),
        "obs_value": gaussian(splits[10], (LEVW, MERIDIAN_CELLS, ZONAL_CELLS, NOBS), 1.0, 6.0, ((0, 2), (1, 16), (2, 8)), jnp.float32),
        "obs_weight": jnp.clip(jnp.exp(math.log(30.0) - 3.4011974 * jax.random.uniform(splits[11], (LEVW, MERIDIAN_CELLS, ZONAL_CELLS, NOBS), jnp.float32) ** levels(splits[11], (LEVW, MERIDIAN_CELLS, ZONAL_CELLS, NOBS), ((0, 2), (1, 16), (2, 8)), -0.2, 0.2)), 1.0, 30.0),
    }


def normalize(tokens):
    values = tokens.astype(jnp.float32)
    center = values - lax.optimization_barrier(jnp.mean(values, axis=-1, keepdims=True))
    spread = lax.optimization_barrier(jnp.mean(center * center, axis=-1, keepdims=True))
    return (center * lax.rsqrt(spread + 1e-05)).astype(jnp.bfloat16)

def feed_forward(hidden_in, w_up, w_down):
    normed = normalize(hidden_in).astype(jnp.float32)
    raised = jnp.einsum('...c,cf->...f', normed, w_up.astype(jnp.float32))
    active = jax.nn.gelu(raised, approximate=False).astype(jnp.bfloat16)
    return jnp.einsum('...f,fc->...c', active.astype(jnp.float32), w_down.astype(jnp.float32))

def batch_product(left_mat, right_mat):
    return jnp.einsum('ijp,jkp->ikp', left_mat, right_mat, precision=lax.Precision.HIGHEST)

def transform(sample_fields, obs_index, obs_count, obs_value, obs_weight):
    member_list = sample_fields.shape[0]
    output_width = sample_fields.shape[3]
    patch_count = sample_fields.shape[2]
    ens_flat = sample_fields.transpose(0, 1, 3, 2).reshape(member_list, -1, patch_count)
    center = lax.optimization_barrier(jnp.mean(ens_flat, axis=0))
    spread = ens_flat - center[None]
    picked = jnp.broadcast_to(obs_index.T[None], (member_list,) + obs_index.T.shape)
    observed = jnp.take_along_axis(ens_flat, picked, axis=1)
    obs_mean = lax.optimization_barrier(jnp.mean(observed, axis=0))
    obs_spread = observed - obs_mean[None]
    slot_ids = jnp.arange(obs_index.shape[1], dtype=jnp.int32)[:, None]
    live_mask = (slot_ids < obs_count[None, :]).astype(jnp.float32)
    weighted = obs_spread * (obs_weight.T * live_mask)[None]
    innovation = obs_value.T - obs_mean
    identity = jnp.eye(member_list, dtype=jnp.float32)[:, :, None]
    matrix = (member_list - 1.0) * identity + jnp.einsum('ikp,jkp->ijp', weighted, obs_spread, precision=lax.Precision.HIGHEST)
    right_side = jnp.einsum('ikp,kp->ip', weighted, innovation, precision=lax.Precision.HIGHEST)
    trace_sum = lax.optimization_barrier(jnp.sum(matrix * identity, axis=(0, 1)))
    iterate = matrix / trace_sum
    inverse_root = jnp.broadcast_to(identity, matrix.shape)
    for sweep_idx in range(NEWTON):
        factor = 1.5 * identity - 0.5 * batch_product(inverse_root, iterate)
        iterate = batch_product(iterate, factor)
        inverse_root = batch_product(factor, inverse_root)
    analysis_cov = batch_product(inverse_root, inverse_root) / trace_sum
    mean_weight = jnp.einsum('ijp,jp->ip', analysis_cov, right_side, precision=lax.Precision.HIGHEST)
    weights = mean_weight[:, None, :] + math.sqrt(member_list - 1.0) * inverse_root * lax.rsqrt(trace_sum)
    updated = center[None] + jnp.einsum('inp,imp->mnp', spread, weights, precision=lax.Precision.HIGHEST)
    return updated.reshape(member_list, VERTICAL_DEPTH, output_width, patch_count).transpose(0, 1, 3, 2)

def run_member(member_state, offset, w_qkv, w_out, w_up, w_down, head_weight, pos_bias):
    half_rows = LAT_DEV // 2
    blocks = (MERIDIAN_CELLS + 2 * half_rows) // LAT_DEV
    lev_win = LEV // VERTICAL_DEPTH
    lon_win = ZONAL_CELLS // WLON
    padded = jnp.pad(member_state, ((0, 0), (half_rows, half_rows), (0, 0), (0, 0)))
    rolled = jnp.roll(padded, -offset, axis=2)
    normed = normalize(rolled)
    windows = normed.reshape(lev_win, VERTICAL_DEPTH, blocks, LAT_DEV, lon_win, WLON, C).transpose(0, 2, 4, 1, 3, 5, 6).reshape(-1, WTOK, C)
    window_count = windows.shape[0]
    packed = jnp.einsum('gpc,cte->gpte', windows.astype(jnp.float32), w_qkv.astype(jnp.float32)).astype(jnp.bfloat16)
    queries = packed[:, :, 0].reshape(window_count, WTOK, HEADS, HEAD_DIM).astype(jnp.float32)
    keys_in = packed[:, :, 1].reshape(window_count, WTOK, HEADS, HEAD_DIM).astype(jnp.float32)
    values_in = packed[:, :, 2].reshape(window_count, WTOK, HEADS, HEAD_DIM).astype(jnp.float32)
    scores = jnp.einsum('gqhd,gkhd->ghqk', queries, keys_in) * HEAD_DIM ** (-0.5)
    scores = scores + pos_bias.astype(jnp.float32)[None]
    lat_pos = jnp.arange(WTOK, dtype=jnp.int32) // WLON % LAT_DEV
    row_global = jnp.arange(blocks, dtype=jnp.int32)[:, None] * LAT_DEV + lat_pos[None, :]
    usable = (row_global >= half_rows) & (row_global < MERIDIAN_CELLS + half_rows)
    usable = jnp.broadcast_to(usable[None, :, None, :], (lev_win, blocks, lon_win, WTOK)).reshape(window_count, WTOK)
    scores = jnp.where(usable[:, None, None, :], scores, -1000000000.0)
    softmaxed = jax.nn.softmax(scores, axis=-1).astype(jnp.bfloat16)
    mixture = jnp.einsum('ghqk,gkhd->gqhd', softmaxed.astype(jnp.float32), values_in).astype(jnp.bfloat16)
    mixture = mixture.reshape(window_count, WTOK, C)
    projected = jnp.einsum('gqe,ec->gqc', mixture.astype(jnp.float32), w_out.astype(jnp.float32))
    restored = projected.reshape(lev_win, blocks, lon_win, VERTICAL_DEPTH, LAT_DEV, WLON, C).transpose(0, 3, 1, 4, 2, 5, 6)
    restored = restored.reshape(LEV, blocks * LAT_DEV, ZONAL_CELLS, C)
    restored = jnp.roll(restored, offset, axis=2)[:, half_rows:half_rows + MERIDIAN_CELLS]
    section_one = member_state.astype(jnp.float32) + restored
    second_section = (section_one + feed_forward(section_one, w_up, w_down)).astype(jnp.bfloat16)
    return jnp.einsum('fngu,uz->fngz', second_section.astype(jnp.float32), head_weight.astype(jnp.float32))

def reference(prior_grids, w_qkv, w_out, w_up, w_down, head_weight, pos_bias, zonal_offsets, obs_index, obs_count, obs_value, obs_weight):

    def predict_one_sample(sample_collection):
        return run_member(sample_collection[0], sample_collection[1], w_qkv, w_out, w_up, w_down, head_weight, pos_bias)
    predict_samples = lax.map(predict_one_sample, (prior_grids, zonal_offsets))
    vertical_couples = LEV // VERTICAL_DEPTH
    divided_pieces = predict_samples.reshape(SAMPLE_COUNT, vertical_couples, VERTICAL_DEPTH, MERIDIAN_CELLS, ZONAL_CELLS, PATCH_PREDICTED).transpose(1, 0, 2, 3, 4, 5)
    divided_pieces = divided_pieces.reshape(vertical_couples, SAMPLE_COUNT, VERTICAL_DEPTH, MERIDIAN_CELLS * ZONAL_CELLS, PATCH_PREDICTED)

    def analyse(sample_collection):
        return transform(sample_collection[0], sample_collection[1], sample_collection[2], sample_collection[3], sample_collection[4])
    result = lax.map(analyse, (divided_pieces, obs_index.reshape(vertical_couples, MERIDIAN_CELLS * ZONAL_CELLS, NOBS), obs_count.reshape(vertical_couples, MERIDIAN_CELLS * ZONAL_CELLS), obs_value.reshape(vertical_couples, MERIDIAN_CELLS * ZONAL_CELLS, NOBS), obs_weight.reshape(vertical_couples, MERIDIAN_CELLS * ZONAL_CELLS, NOBS)))
    result = result.reshape(vertical_couples, SAMPLE_COUNT, VERTICAL_DEPTH, MERIDIAN_CELLS, ZONAL_CELLS, PATCH_PREDICTED).transpose(1, 0, 2, 3, 4, 5)
    return result.reshape(SAMPLE_COUNT, LEV, MERIDIAN_CELLS, ZONAL_CELLS, PATCH_PREDICTED)
```

```python
import functools
import math

import jax
import jax.numpy as jnp
from jax import lax
from jax.experimental import pallas as pl
from jax.experimental.pallas import tpu as pltpu
from jax.sharding import PartitionSpec as P

F32 = jnp.float32
BF16 = jnp.bfloat16
MESH = pl.DeviceIdType.MESH
C = 192
FF = 768
NV = 160
NEWTON = 8
MEMBERS = 8
BANDS = 16
LOG2E = 1.4426950408889634


def nt(a, b):
    return lax.dot_general(a, b, (((1,), (1,)), ((), ())), preferred_element_type=F32)


def nn(a, b):
    return jnp.dot(a, b, preferred_element_type=F32)


def iota(shape, dim):
    return lax.broadcasted_iota(jnp.int32, shape, dim)


def onehot(cond):
    return jnp.where(cond, 1.0, 0.0).astype(BF16)


def eye(n):
    return onehot(iota((n, n), 0) == iota((n, n), 1))


def gelu(x):
    return 0.5 * x * (1.0 + lax.erf(x * 0.7071067811865476))


def forecast_kernel(
    off_ref,
    prior,
    wqkv_in,
    wout_in,
    wup_in,
    wdown_in,
    bias_in,
    head_in,
    out,
    xown,
    halo,
    wqkv,
    wout,
    wup,
    wdown,
    bias,
    head,
    wout_t,
    wup_t,
    wdown_t,
    head_t,
    biasl,
    perm,
    sendperm,
    nbuf,
    xbuf,
    kbuf,
    vbuf,
    qbuf,
    mixbuf,
    fbuf,
    sendbuf,
    local_sem,
    halo_send,
    halo_recv,
    w_send,
    w_recv,
    f_send,
    f_recv,
    a_send,
    a_recv,
    a_local,
):
    member = lax.axis_index("member")
    band = lax.axis_index("band")
    tensor = lax.axis_index("tensor")
    parity = lax.rem(band, 2)
    other = 1 - tensor
    sibling = band + 1 - 2 * parity
    far = lax.rem(band + 2 * parity - 1 + BANDS, BANDS)
    xband = lax.rem(band + BANDS // 2, BANDS)
    side = (1 - parity, parity)

    barrier = pltpu.get_barrier_semaphore()
    pl.semaphore_signal(barrier, inc=1, device_id={"band": sibling}, device_id_type=MESH)
    pl.semaphore_signal(barrier, inc=1, device_id={"band": far}, device_id_type=MESH)
    pl.semaphore_signal(
        barrier, inc=1, device_id={"band": xband, "tensor": other}, device_id_type=MESH
    )
    for k in range(1, MEMBERS):
        pl.semaphore_signal(
            barrier,
            inc=1,
            device_id={"member": lax.rem(member + k, MEMBERS)},
            device_id_type=MESH,
        )

    def part(ref, i, half, c):
        if i == 0:
            return ref.at[:, half, pl.ds(c * 48, 48)]
        if i == 1:
            return ref.at[half, :, pl.ds(c * 64, 64)]
        if i == 2:
            return ref.at[half, pl.ds(c * 48, 48)]
        if i == 3:
            return ref.at[half, pl.ds(c * 96, 96)]
        return ref.at[half, pl.ds(c * 192, 192)]

    def src_part(ref, i, c):
        if i == 0:
            return ref.at[:, pl.ds(c * 48, 48)]
        if i == 1:
            return ref.at[:, pl.ds(c * 64, 64)]
        if i == 2:
            return ref.at[pl.ds(c * 48, 48)]
        if i == 3:
            return ref.at[pl.ds(c * 96, 96)]
        return ref.at[pl.ds(c * 192, 192)]

    sources = (wqkv_in, bias_in, wout_in, wup_in, wdown_in)
    targets = (wqkv, bias, wout, wup, wdown)

    own_x = pltpu.make_async_copy(
        prior.at[0, pl.ds(2 * tensor, 2)], xown, local_sem.at[0]
    )
    own_x.start()
    locals_ = []
    for i in range(5):
        dst = targets[i].at[:, tensor] if i == 0 else targets[i].at[tensor]
        locals_.append(pltpu.make_async_copy(sources[i], dst, local_sem.at[1 + i]))
    locals_.append(pltpu.make_async_copy(head_in, head, local_sem.at[6]))
    for copy in locals_:
        copy.start()

    pl.semaphore_wait(barrier, 3 + MEMBERS - 1)

    halos = []
    for ph, peer in ((0, sibling), (1, far)):
        halos.append(
            pltpu.make_async_remote_copy(
                src_ref=prior.at[0, pl.ds(2 * tensor, 2), pl.ds(4 * side[ph], 4)],
                dst_ref=halo.at[ph],
                send_sem=halo_send.at[ph],
                recv_sem=halo_recv.at[ph],
                device_id={"band": peer},
                device_id_type=MESH,
            )
        )
    weights = []
    forwards = []
    for i in range(5):
        weights.append(
            pltpu.make_async_remote_copy(
                src_ref=src_part(sources[i], i, parity),
                dst_ref=part(targets[i], i, tensor, parity),
                send_sem=w_send.at[i],
                recv_sem=w_recv.at[i],
                device_id={"band": xband, "tensor": other},
                device_id_type=MESH,
            )
        )
        piece = part(targets[i], i, other, parity)
        forwards.append(
            pltpu.make_async_remote_copy(
                src_ref=piece,
                dst_ref=piece,
                send_sem=f_send.at[i],
                recv_sem=f_recv.at[i],
                device_id={"band": sibling},
                device_id_type=MESH,
            )
        )
    weights[0].start()
    halos[0].start()
    halos[1].start()
    for i in range(1, 5):
        weights[i].start()

    offset = off_ref[0]
    row_i = iota((256, 256), 0)
    col_i = iota((256, 256), 1)
    place = jnp.bitwise_and((row_i // 16) * 8 + jnp.bitwise_and(row_i, 7) + offset, 127)
    want = jnp.bitwise_and(row_i // 8, 1) * 128 + place
    perm[...] = onehot(want == col_i)

    def build_send(i, _):
        rows = iota((64, 1024), 0)
        cols = iota((64, 1024), 1)
        level = jnp.bitwise_and(rows // 8, 1)
        row = rows // 16
        where = jnp.bitwise_and(i * 8 + jnp.bitwise_and(rows, 7) + offset, 127)
        target = (where // 16) * 128 + level * 64 + row * 16 + jnp.bitwise_and(where, 15)
        sendperm[pl.ds(pl.multiple_of(i * 64, 64), 64), :] = onehot(target == cols)
        return 0

    lax.fori_loop(0, 16, build_send, 0)

    def prepare(block, ph, slot, keep):
        moved = nn(perm[...], block)
        mean = jnp.sum(moved, axis=1, keepdims=True) * (1.0 / C)
        center = moved - mean
        spread = jnp.sum(center * center, axis=1, keepdims=True) * (1.0 / C)
        normed = (center * lax.rsqrt(spread + 1e-05)).astype(BF16)
        nbuf[ph, :, slot] = normed.reshape(16, 16, C)
        if keep:
            xbuf[ph, :, slot] = moved.astype(BF16).reshape(16, 16, C)

    own_x.wait()
    for ph in range(2):

        def own_row(r, _, ph=ph):
            row = 4 * side[ph] + r
            block = jnp.concatenate([xown[0, row], xown[1, row]], axis=0)
            prepare(block, ph, r, True)
            return 0

        lax.fori_loop(0, 4, own_row, 0)

    for copy in locals_:
        copy.wait()
    weights[0].wait()
    forwards[0].start()
    halos[0].wait()

    def halo_rows(ph):
        def body(r, _):
            block = jnp.concatenate([halo[ph, 0, r], halo[ph, 1, r]], axis=0)
            prepare(block, ph, 4 + r, False)
            return 0

        lax.fori_loop(0, 4, body, 0)

    halo_rows(0)
    for i in range(1, 5):
        weights[i].wait()
        forwards[i].start()
    for i in range(5):
        forwards[i].wait()

    wout_t[...] = nt(eye(C), wout[...].reshape(C, C)).astype(BF16)
    for half in range(2):
        wup_t[half * 384 : half * 384 + 384, :] = nt(eye(384), wup[half]).astype(BF16)
        wdown_t[:, half * 384 : half * 384 + 384] = nt(eye(C), wdown[half]).astype(BF16)
    head_t[...] = nt(eye(NV), head[...]).astype(BF16)

    key_i = iota((128, 128), 0)
    pos_i = iota((128, 128), 1)
    edge = jnp.logical_or(band == 0, band == BANDS - 1)
    for ph in range(2):
        turn = 4 * (1 - side[ph])

        def position(index):
            row = jnp.bitwise_and(index // 16 + turn, 7)
            return (jnp.bitwise_and(index // 8, 1) * 8 + row) * 8 + jnp.bitwise_and(index, 7)

        keys_sel = onehot(position(key_i) == pos_i)
        first = onehot(jnp.logical_and(position(key_i) == pos_i, key_i < 64))
        second = onehot(jnp.logical_and(position(key_i - 64) == pos_i, key_i >= 64))
        for t in range(3):
            turned = []
            for h in (2 * t, 2 * t + 1):
                turned.append(nt(keys_sel, bias[h // 3, h % 3]).astype(BF16))
            for w in range(2):
                lo, hi = (turned[0], turned[1]) if w == 0 else (turned[1], turned[0])
                value = (nt(lo, first) + nt(hi, second)) * LOG2E
                if ph == 1:
                    value = jnp.where(jnp.logical_and(edge, key_i >= 64), -1e9, value)
                biasl[ph, w, t] = value

    lane = iota((1, 128), 1)
    low = lane < 64
    zero64 = jnp.zeros((64, 128), BF16)
    ones16 = jnp.ones((16, 128), BF16)

    def phase(ph):
        wq = wqkv[0].reshape(C, C)
        wk = wqkv[1].reshape(C, C)
        wv = wqkv[2].reshape(C, C)

        def project(j, _):
            tokens = nbuf[ph, pl.ds(4 * j, 4)].reshape(512, C)
            own = nbuf[ph, pl.ds(4 * j, 4), 0:4].reshape(256, C)
            kbuf[pl.ds(pl.multiple_of(512 * j, 512), 512), :] = nt(tokens, wk).astype(BF16)
            v = nt(wv, tokens).astype(BF16)
            for i in range(2):
                vbuf[2 * j + i] = v[:, 256 * i : 256 * i + 256]
            q = nt(wq, own)
            for i in range(2):
                qbuf[2 * j + i] = q[:, 128 * i : 128 * i + 128].astype(BF16)
            return 0

        lax.fori_loop(0, 4, project, 0)

        def window_pair(j, _):
            keys = kbuf[pl.ds(pl.multiple_of(256 * j, 256), 256), :]
            values = vbuf[j]
            queries = qbuf[j].astype(F32)
            lows = []
            highs = []
            for h in range(6):
                q = queries[32 * h : 32 * h + 32]
                if h % 2:
                    q = pltpu.roll(q, 64, 1)
                lows.append(jnp.where(low, q, 0.0).astype(BF16))
                highs.append(jnp.where(low, 0.0, q).astype(BF16))
            results = []
            for w in range(2):
                even, odd = (lows, highs) if w == 0 else (highs, lows)
                columns = []
                for t in range(3):
                    pieces = [zero64] * 3
                    pieces[t] = jnp.concatenate([even[2 * t], odd[2 * t + 1]], axis=0)
                    columns.append(jnp.concatenate(pieces, axis=0))
                stacked = jnp.concatenate(columns, axis=1)
                scores = nn(keys[128 * w : 128 * w + 128], stacked)
                result = []
                for t in range(3):
                    s = scores[:, 128 * t : 128 * t + 128] * (LOG2E * 32**-0.5)
                    s = s + biasl[ph, w, t]
                    s = s - jnp.max(s, axis=0, keepdims=True)
                    probs = jnp.exp2(s).astype(BF16)
                    left = jnp.concatenate(
                        [values[64 * t : 64 * t + 64, 128 * w : 128 * w + 128], ones16], axis=0
                    )
                    result.append(nn(left, probs))
                results.append(result)
            rows = []
            for t in range(3):
                a, b = results[0][t], results[1][t]
                even = jnp.where(low, a[0:32], b[0:32])
                even = even / jnp.where(low, a[64:65], b[64:65])
                odd = jnp.where(low, b[32:64], a[32:64])
                odd = odd / jnp.where(low, b[64:65], a[64:65])
                rows.append(even)
                rows.append(pltpu.roll(odd, 64, 1))
            mixbuf[:, pl.ds(pl.multiple_of(128 * j, 128), 128)] = jnp.concatenate(
                rows, axis=0
            ).astype(BF16)
            return 0

        lax.fori_loop(0, 8, window_pair, 0)

        def mlp(j, _):
            cols = pl.ds(pl.multiple_of(256 * j, 256), 256)
            prior_t = nt(eye(C), xbuf[ph, pl.ds(4 * j, 4)].reshape(256, C))
            one = prior_t + nn(wout_t[...], mixbuf[:, cols])
            mean = jnp.sum(one, axis=0, keepdims=True) * (1.0 / C)
            center = one - mean
            spread = jnp.sum(center * center, axis=0, keepdims=True) * (1.0 / C)
            normed = (center * lax.rsqrt(spread + 1e-05)).astype(BF16)
            active = gelu(nn(wup_t[...], normed)).astype(BF16)
            two = (one + nn(wdown_t[...], active)).astype(BF16)
            fbuf[:, cols] = nn(head_t[...], two).astype(BF16)
            return 0

        lax.fori_loop(0, 4, mlp, 0)

        sent = nn(fbuf[...], sendperm[...])
        for d in range(MEMBERS):
            sendbuf[ph, d] = sent[:, 128 * d : 128 * d + 128].astype(BF16)
        copies = []
        for k in range(1, MEMBERS):
            to = lax.rem(member + k, MEMBERS)
            copies.append(
                pltpu.make_async_remote_copy(
                    src_ref=sendbuf.at[ph, to],
                    dst_ref=out.at[ph, member],
                    send_sem=a_send.at[ph, k],
                    recv_sem=a_recv.at[ph, k],
                    device_id={"member": to},
                    device_id_type=MESH,
                )
            )
        mine = pltpu.make_async_copy(sendbuf.at[ph, member], out.at[ph, member], a_local.at[ph])
        for copy in copies:
            copy.start()
        mine.start()
        return copies + [mine]

    pending = phase(0)
    halos[1].wait()
    halo_rows(1)
    pending = pending + phase(1)
    for copy in pending:
        copy.wait()


def forecast(off, prior, wqkv, wout, wup, wdown, bias, head):
    vmem = pltpu.VMEM
    dma = pltpu.SemaphoreType.DMA
    hbm = pl.BlockSpec(memory_space=pl.ANY)
    return pl.pallas_call(
        forecast_kernel,
        out_shape=jax.ShapeDtypeStruct((2, MEMBERS, NV, 128), BF16),
        in_specs=[pl.BlockSpec(memory_space=pltpu.SMEM)] + [hbm] * 7,
        out_specs=hbm,
        scratch_shapes=[
            vmem((2, 8, 128, C), BF16),
            vmem((2, 2, 4, 128, C), BF16),
            vmem((3, 2, 96, C), BF16),
            vmem((2, 96, C), BF16),
            vmem((2, C, 384), BF16),
            vmem((2, 384, C), BF16),
            vmem((2, 3, 128, 128), BF16),
            vmem((C, NV), BF16),
            vmem((C, C), BF16),
            vmem((FF, C), BF16),
            vmem((C, FF), BF16),
            vmem((NV, C), BF16),
            vmem((2, 2, 3, 128, 128), F32),
            vmem((256, 256), BF16),
            vmem((1024, 1024), BF16),
            vmem((2, 16, 8, 16, C), BF16),
            vmem((2, 16, 4, 16, C), BF16),
            vmem((2048, C), BF16),
            vmem((8, C, 256), BF16),
            vmem((8, C, 128), BF16),
            vmem((C, 1024), BF16),
            vmem((NV, 1024), BF16),
            vmem((2, MEMBERS, NV, 128), BF16),
            dma((7,)),
            dma((2,)),
            dma((2,)),
            dma((5,)),
            dma((5,)),
            dma((5,)),
            dma((5,)),
            dma((2, MEMBERS)),
            dma((2, MEMBERS)),
            dma((2,)),
        ],
        compiler_params=pltpu.CompilerParams(
            collective_id=0, has_side_effects=True, vmem_limit_bytes=48 * 1024 * 1024
        ),
        cost_estimate=pl.CostEstimate(
            flops=3_000_000_000, bytes_accessed=6_000_000, transcendentals=3_200_000
        ),
        name="forecast",
    )(off, prior, wqkv, wout, wup, wdown, bias, head)


def analysis_kernel(recv, index, count, value, weight, out, xf, vt):
    parity = lax.rem(lax.axis_index("band"), 2)
    eye128 = eye(128)
    for ph in range(2):
        base = 4 * (1 - parity) if ph == 0 else 4 * parity
        for m in range(MEMBERS):
            x = nt(eye128, recv[ph, m])
            xf[m, :, pl.ds(base, 4), :, 0:NV] = x.reshape(2, 4, 16, NV)

    lane = iota((128, 128), 1)
    pad = jnp.zeros((128, 112), jnp.int32)
    spread_index = jnp.concatenate([index[0].reshape(128, 16), pad], axis=1)
    idx = jnp.take_along_axis(spread_index, lane // 8, axis=1, mode="promise_in_bounds")
    level = idx >= NV
    inner = jnp.where(level, idx - NV, idx)
    upper = inner >= 128
    inner = jnp.bitwise_and(inner, 127)
    slot_member = jnp.bitwise_and(lane, 7)
    observed = jnp.zeros((128, 128), F32)
    for m in range(MEMBERS):
        picks = []
        for a in range(2):
            for part in range(2):
                x = xf[m, a, :, :, 128 * part : 128 * part + 128].reshape(128, 128)
                picks.append(jnp.take_along_axis(x, inner, axis=1, mode="promise_in_bounds"))
        got = jnp.where(
            level,
            jnp.where(upper, picks[3], picks[2]),
            jnp.where(upper, picks[1], picks[0]),
        )
        observed = jnp.where(slot_member == m, got, observed)
    obs_t = observed.T

    blank = jnp.zeros((128, 96), F32)
    terms = jnp.concatenate(
        [value[0].reshape(128, 16), weight[0].reshape(128, 16), blank], axis=1
    ).T
    counts = count[0].astype(F32).astype(BF16)
    spread = onehot(iota((16, 128), 0) == jnp.bitwise_and(iota((16, 128), 1), 15))
    wide = nn(counts, spread)
    live_count = jnp.sum(
        jnp.where(iota((8, 128), 0) == iota((8, 128), 1) // 16, wide, 0.0), axis=0, keepdims=True
    )

    sub = iota((8, 128), 0)
    rows = [jnp.zeros((8, 128), F32) for _ in range(MEMBERS)]
    right = jnp.zeros((8, 128), F32)
    for k in range(16):
        y = obs_t[8 * k : 8 * k + 8]
        mean = jnp.sum(y, axis=0, keepdims=True) * (1.0 / MEMBERS)
        dev = y - mean
        r = jnp.where(live_count > k, terms[16 + k : 17 + k], 0.0)
        scaled = dev * r
        right = right + scaled * (terms[k : k + 1] - mean)
        for i in range(MEMBERS):
            rows[i] = rows[i] + scaled[i : i + 1] * dev
    for i in range(MEMBERS):
        rows[i] = rows[i] + jnp.where(sub == i, MEMBERS - 1.0, 0.0)
    diagonal = jnp.zeros((8, 128), F32)
    for i in range(MEMBERS):
        diagonal = diagonal + jnp.where(sub == i, rows[i], 0.0)
    trace = jnp.sum(diagonal, axis=0, keepdims=True)
    inverse_trace = 1.0 / trace
    g = [row * inverse_trace for row in rows]

    def product(left, right_mat):
        result = []
        for i in range(MEMBERS):
            total = left[i][0:1] * right_mat[0]
            for j in range(1, MEMBERS):
                total = total + left[i][j : j + 1] * right_mat[j]
            result.append(total)
        return result

    def factor_of(zg):
        return [jnp.where(sub == i, 1.5, 0.0) - 0.5 * zg[i] for i in range(MEMBERS)]

    f = factor_of(g)
    g = product(g, f)
    z = f
    for step in range(1, NEWTON):
        f = factor_of(product(z, g))
        if step < NEWTON - 1:
            g = product(g, f)
        z = product(f, z)

    def apply(mat, vec):
        total = mat[0] * vec[0:1]
        for j in range(1, MEMBERS):
            total = total + mat[j] * vec[j : j + 1]
        return total

    wbar = apply(z, apply(z, right)) * inverse_trace
    scale = math.sqrt(MEMBERS - 1.0) * lax.rsqrt(trace)
    full = [wbar[i : i + 1] + z[i] * scale for i in range(MEMBERS)]
    mean_row = full[0]
    for i in range(1, MEMBERS):
        mean_row = mean_row + full[i]
    shift = (1.0 - mean_row) * (1.0 / MEMBERS)
    final = jnp.concatenate([row + shift for row in full] + [jnp.zeros((64, 128), F32)], axis=0)
    vt[...] = final.T

    def update(p, _):
        row = p // 2
        half = pl.ds(pl.multiple_of(jnp.bitwise_and(p, 1) * 8, 8), 8)
        coeff = vt[pl.ds(pl.multiple_of(p * 8, 8), 8), :]
        for a in range(2):
            x = [xf[i, a, row, half, :] for i in range(MEMBERS)]
            for m in range(MEMBERS):
                total = coeff[:, m : m + 1] * x[0]
                for i in range(1, MEMBERS):
                    total = total + coeff[:, 8 * i + m : 8 * i + m + 1] * x[i]
                out[m, a, row, half, :] = total[:, 0:NV]
        return 0

    lax.fori_loop(0, 16, update, 0)


def analyse(recv, index, count, value, weight):
    return pl.pallas_call(
        analysis_kernel,
        out_shape=jax.ShapeDtypeStruct((MEMBERS, 2, 8, 16, NV), F32),
        scratch_shapes=[
            pltpu.VMEM((MEMBERS, 2, 8, 16, 256), F32),
            pltpu.VMEM((128, 128), F32),
        ],
        compiler_params=pltpu.CompilerParams(vmem_limit_bytes=48 * 1024 * 1024),
        cost_estimate=pl.CostEstimate(
            flops=20_000_000, bytes_accessed=3_000_000, transcendentals=0
        ),
        name="analyse",
    )(recv, index, count, value, weight)


def shards(
    prior_grids,
    w_qkv,
    w_out,
    w_up,
    w_down,
    head_weight,
    pos_bias,
    zonal_offsets,
    obs_index,
    obs_count,
    obs_value,
    obs_weight,
):
    recv = forecast(
        zonal_offsets,
        prior_grids,
        w_qkv.transpose(1, 2, 0),
        w_out,
        w_up,
        w_down,
        pos_bias,
        head_weight,
    )
    return analyse(recv, obs_index, obs_count, obs_value, obs_weight)


def solution(mesh):
    return jax.shard_map(
        shards,
        mesh=mesh,
        in_specs=(
            P("member", None, "band", None, None),
            P(None, None, "tensor"),
            P("tensor", None),
            P(None, "tensor"),
            P("tensor", None),
            P(),
            P("tensor", None, None),
            P("member"),
            P("tensor", "band", "member", None),
            P("tensor", "band", "member"),
            P("tensor", "band", "member", None),
            P("tensor", "band", "member", None),
        ),
        out_specs=P(None, "tensor", "band", "member", None),
        check_vma=False,
    )
```

```python
import functools
import math

import jax
import jax.numpy as jnp
from jax import lax
from jax.experimental import pallas as pl
from jax.experimental.pallas import tpu as pltpu
from jax.sharding import PartitionSpec as P

F32 = jnp.float32
BF16 = jnp.bfloat16
MESH = pl.DeviceIdType.MESH
C = 192
FF = 768
NV = 160
NEWTON = 8
MEMBERS = 8
BANDS = 16
LOG2E = 1.4426950408889634


def nt(a, b):
    return lax.dot_general(a, b, (((1,), (1,)), ((), ())), preferred_element_type=F32)


def nn(a, b):
    return jnp.dot(a, b, preferred_element_type=F32)


def iota(shape, dim):
    return lax.broadcasted_iota(jnp.int32, shape, dim)


def onehot(cond):
    return jnp.where(cond, 1.0, 0.0).astype(BF16)


def eye(n):
    return onehot(iota((n, n), 0) == iota((n, n), 1))


def gelu(x):
    return 0.5 * x * (1.0 + lax.erf(x * 0.7071067811865476))


def forecast_kernel(
    off_ref,
    prior,
    wqkv_in,
    wout_in,
    wup_in,
    wdown_in,
    bias_in,
    head_in,
    out,
    xown,
    halo,
    wqkv,
    wout,
    wup,
    wdown,
    bias,
    head_t,
    wqkv_t,
    wout_t,
    wup_t,
    biasl,
    perm,
    sendperm,
    nbuf,
    xbuf,
    kbuf,
    vbuf,
    qbuf,
    sbuf,
    pbuf,
    mixbuf,
    onebuf,
    nextbuf,
    actbuf,
    fbuf,
    sendbuf,
    local_sem,
    halo_send,
    halo_recv,
    w_send,
    w_recv,
    f_send,
    f_recv,
    a_send,
    a_recv,
    a_local,
):
    member = lax.axis_index("member")
    band = lax.axis_index("band")
    tensor = lax.axis_index("tensor")
    parity = lax.rem(band, 2)
    other = 1 - tensor
    sibling = band + 1 - 2 * parity
    far = lax.rem(band + 2 * parity - 1 + BANDS, BANDS)
    xband = lax.rem(band + BANDS // 2, BANDS)
    side = (1 - parity, parity)

    barrier = pltpu.get_barrier_semaphore()
    pl.semaphore_signal(barrier, inc=1, device_id={"band": sibling}, device_id_type=MESH)
    pl.semaphore_signal(barrier, inc=1, device_id={"band": far}, device_id_type=MESH)
    pl.semaphore_signal(
        barrier, inc=1, device_id={"band": xband, "tensor": other}, device_id_type=MESH
    )
    for k in range(1, MEMBERS):
        pl.semaphore_signal(
            barrier,
            inc=1,
            device_id={"member": lax.rem(member + k, MEMBERS)},
            device_id_type=MESH,
        )

    def part(ref, i, half, c):
        if i == 0:
            return ref.at[half, :, pl.ds(c * 96, 96)]
        if i == 1:
            return ref.at[half, :, pl.ds(c * 64, 64)]
        if i == 2:
            return ref.at[half, pl.ds(c * 48, 48)]
        return ref.at[half, pl.ds(c * 96, 96)]

    def src_part(ref, i, c):
        if i == 0:
            return ref.at[:, pl.ds(c * 96, 96)]
        if i == 1:
            return ref.at[:, pl.ds(c * 64, 64)]
        if i == 2:
            return ref.at[pl.ds(c * 48, 48)]
        return ref.at[pl.ds(c * 96, 96)]

    sources = (wqkv_in, bias_in, wout_in, wup_in, wdown_in)
    targets = (wqkv, bias, wout, wup, wdown)

    own_x = pltpu.make_async_copy(
        prior.at[0, pl.ds(2 * tensor, 2)], xown, local_sem.at[0]
    )
    own_x.start()
    locals_ = []
    for i in range(5):
        locals_.append(
            pltpu.make_async_copy(sources[i], targets[i].at[tensor], local_sem.at[1 + i])
        )
    locals_.append(pltpu.make_async_copy(head_in, head_t, local_sem.at[6]))
    for copy in locals_:
        copy.start()

    offset = off_ref[0]
    row_i = iota((256, 256), 0)
    col_i = iota((256, 256), 1)
    place = jnp.bitwise_and((row_i // 16) * 8 + jnp.bitwise_and(row_i, 7) + offset, 127)
    want = jnp.bitwise_and(row_i // 8, 1) * 128 + place
    perm[...] = onehot(want == col_i)

    def build_send(i, _):
        rows = iota((64, 1024), 0)
        cols = iota((64, 1024), 1)
        level = jnp.bitwise_and(rows // 8, 1)
        row = rows // 16
        where = jnp.bitwise_and(i * 8 + jnp.bitwise_and(rows, 7) + offset, 127)
        target = (where // 16) * 128 + level * 64 + row * 16 + jnp.bitwise_and(where, 15)
        sendperm[pl.ds(pl.multiple_of(i * 64, 64), 64), :] = onehot(target == cols)
        return 0

    pl.semaphore_wait(barrier, 3 + MEMBERS - 1)

    halos = []
    for ph, peer in ((0, sibling), (1, far)):
        halos.append(
            pltpu.make_async_remote_copy(
                src_ref=prior.at[0, pl.ds(2 * tensor, 2), pl.ds(4 * side[ph], 4)],
                dst_ref=halo.at[ph],
                send_sem=halo_send.at[ph],
                recv_sem=halo_recv.at[ph],
                device_id={"band": peer},
                device_id_type=MESH,
            )
        )
    weights = []
    forwards = []
    for i in range(5):
        weights.append(
            pltpu.make_async_remote_copy(
                src_ref=src_part(sources[i], i, parity),
                dst_ref=part(targets[i], i, tensor, parity),
                send_sem=w_send.at[i],
                recv_sem=w_recv.at[i],
                device_id={"band": xband, "tensor": other},
                device_id_type=MESH,
            )
        )
        piece = part(targets[i], i, other, parity)
        forwards.append(
            pltpu.make_async_remote_copy(
                src_ref=piece,
                dst_ref=piece,
                send_sem=f_send.at[i],
                recv_sem=f_recv.at[i],
                device_id={"band": sibling},
                device_id_type=MESH,
            )
        )
    weights[0].start()
    halos[0].start()
    weights[1].start()
    halos[1].start()
    for i in range(2, 5):
        weights[i].start()

    def prepare(block, ph, slot, keep):
        tokens = block.astype(F32)
        mean = jnp.sum(tokens, axis=0, keepdims=True) * (1.0 / C)
        center = tokens - mean
        spread = jnp.sum(center * center, axis=0, keepdims=True) * (1.0 / C)
        normed = (center * lax.rsqrt(spread + 1e-05)).astype(BF16)
        nbuf[ph, :, slot] = nt(perm[...], normed).astype(BF16).reshape(16, 16, C)
        if keep:
            xbuf[ph, :, slot] = nt(perm[...], block).astype(BF16).reshape(16, 16, C)

    own_x.wait()
    for ph in range(2):
        for r in range(4):
            row = 4 * side[ph] + r
            prepare(jnp.concatenate([xown[0, row], xown[1, row]], axis=1), ph, r, True)

    def halo_rows(ph):
        for r in range(4):
            prepare(jnp.concatenate([halo[ph, 0, r], halo[ph, 1, r]], axis=1), ph, 4 + r, False)

    lax.fori_loop(0, 16, build_send, 0)
    for copy in locals_:
        copy.wait()
    weights[0].wait()
    forwards[0].start()
    halos[0].wait()
    halo_rows(0)
    weights[1].wait()
    forwards[1].start()
    forwards[0].wait()

    for half in range(2):
        for i in range(3):
            turned = nt(eye(96), wqkv[half, i]).astype(BF16)
            if i > 0:
                wqkv_t[i, half * 96 : half * 96 + 96] = turned
                continue
            for n in range(3):
                h = 3 * half + n
                to = (h // 2) * 32 + (h % 2) * 96
                wqkv_t[0, to : to + 32] = turned[32 * n : 32 * n + 32]

    lane = iota((1, 128), 1)
    low = lane < 64

    def project(ph):
        wk, wv = wqkv_t[1], wqkv_t[2]
        wq_even, wq_odd = wqkv_t[0, 0:96], wqkv_t[0, 96:192]
        wide_low = jnp.bitwise_and(iota((1, 256), 1), 127) < 64
        for j in range(4):
            tokens = nbuf[ph, 4 * j : 4 * j + 4].reshape(512, C)
            own = nbuf[ph, 4 * j : 4 * j + 4, 0:4].reshape(4, 64, C)
            swapped = jnp.concatenate([own[1], own[0], own[3], own[2]], axis=0)
            kbuf[512 * j : 512 * j + 512, :] = nt(tokens, wk).astype(BF16)
            v = nt(wv, tokens).astype(BF16)
            q = jnp.concatenate([nt(wq_even, own.reshape(256, C)), nt(wq_odd, swapped)], axis=0)
            lows = jnp.where(wide_low, q, 0.0).astype(BF16)
            highs = jnp.where(wide_low, 0.0, q).astype(BF16)
            for i in range(2):
                vbuf[2 * j + i] = v[:, 256 * i : 256 * i + 256]
                qbuf[2 * j + i, 0] = lows[:, 128 * i : 128 * i + 128]
                qbuf[2 * j + i, 1] = highs[:, 128 * i : 128 * i + 128]

    zero64 = jnp.zeros((64, 128), BF16)
    ones16 = jnp.ones((16, 128), BF16)

    def attend(ph):
        def step(i, _):
            j = jnp.clip(i - 2, 0, 7)
            results = []
            for w in range(2):
                result = []
                for t in range(3):
                    left = jnp.concatenate(
                        [vbuf[j, 64 * t : 64 * t + 64, 128 * w : 128 * w + 128], ones16], axis=0
                    )
                    result.append(nn(left, pbuf[w, :, 128 * t : 128 * t + 128]))
                results.append(result)
            where = pl.ds(pl.multiple_of(128 * j, 128), 128)
            for t in range(3):
                a, b = results[0][t], results[1][t]
                even = jnp.where(low, a[0:32], b[0:32])
                even = even * (1.0 / jnp.where(low, a[64:65], b[64:65]))
                odd = jnp.where(low, b[32:64], a[32:64])
                odd = odd * (1.0 / jnp.where(low, b[64:65], a[64:65]))
                mixbuf[32 * t : 32 * t + 32, where] = even.astype(BF16)
                mixbuf[96 + 32 * t : 128 + 32 * t, where] = odd.astype(BF16)

            for w in range(2):
                for t in range(3):
                    s = sbuf[w, :, 128 * t : 128 * t + 128] * (LOG2E * 32**-0.5)
                    s = s + biasl[ph, w, t]
                    s = s - jnp.max(s, axis=0, keepdims=True)
                    pbuf[w, :, 128 * t : 128 * t + 128] = jnp.exp2(s).astype(BF16)

            j = jnp.minimum(i, 7)
            for w in range(2):
                columns = []
                for t in range(3):
                    pieces = [zero64] * 3
                    pieces[t] = jnp.concatenate(
                        [
                            qbuf[j, w, 32 * t : 32 * t + 32],
                            qbuf[j, 1 - w, 96 + 32 * t : 128 + 32 * t],
                        ],
                        axis=0,
                    )
                    columns.append(jnp.concatenate(pieces, axis=0))
                start = pl.multiple_of(256 * j + 128 * w, 128)
                sbuf[w] = nn(kbuf[pl.ds(start, 128), :], jnp.concatenate(columns, axis=1))
            return 0

        lax.fori_loop(0, 10, step, 0)

    def mlp(ph):
        def first(j):
            cols = slice(256 * j, 256 * j + 256)
            prior_t = nt(eye(C), xbuf[ph, 4 * j : 4 * j + 4].reshape(256, C))
            odd = mixbuf[96:192, cols].astype(F32)
            odd = jnp.concatenate(
                [pltpu.roll(odd[:, 0:128], 64, 1), pltpu.roll(odd[:, 128:256], 64, 1)], axis=1
            ).astype(BF16)
            mixed = jnp.concatenate([mixbuf[0:96, cols], odd], axis=0)
            one = prior_t + nn(wout_t[...], mixed)
            onebuf[:, cols] = one
            mean = jnp.sum(one, axis=0, keepdims=True) * (1.0 / C)
            center = one - mean
            spread = jnp.sum(center * center, axis=0, keepdims=True) * (1.0 / C)
            nextbuf[:, cols] = (center * lax.rsqrt(spread + 1e-05)).astype(BF16)

        def second(j):
            cols = slice(256 * j, 256 * j + 256)
            actbuf[:, cols] = gelu(nn(wup_t[...], nextbuf[:, cols])).astype(BF16)

        def third(j):
            cols = slice(256 * j, 256 * j + 256)
            raised = nn(wdown[0], actbuf[0:384, cols]) + nn(wdown[1], actbuf[384:768, cols])
            two = (onebuf[:, cols] + raised).astype(BF16)
            fbuf[:, cols] = nn(head_t[...], two).astype(BF16)

        for j in range(6):
            if 0 <= j - 2 < 4:
                third(j - 2)
            if 0 <= j - 1 < 4:
                second(j - 1)
            if j < 4:
                first(j)

    half_member = member // 2
    odd_member = lax.rem(member, 2)

    def send(ph):
        copies = []
        for k in (2, 1, 3, 0):
            pair = lax.rem(half_member + k, 4)
            cols = pl.ds(pl.multiple_of(256 * pair, 256), 256)
            sent = nn(fbuf[...], sendperm[:, cols]).astype(BF16)
            for j in range(2):
                sendbuf[ph, 2 * pair + j] = sent[:, 128 * j : 128 * j + 128]
            for j in range(2):
                to = 2 * pair + j
                if k == 0:
                    if j == 1:
                        continue
                    to = member + 1 - 2 * odd_member
                copy = pltpu.make_async_remote_copy(
                    src_ref=sendbuf.at[ph, to],
                    dst_ref=out.at[ph, member],
                    send_sem=a_send.at[ph, 2 * k + j],
                    recv_sem=a_recv.at[ph, 2 * k + odd_member],
                    device_id={"member": to},
                    device_id_type=MESH,
                )
                copy.start()
                copies.append(copy)
        mine = pltpu.make_async_copy(sendbuf.at[ph, member], out.at[ph, member], a_local.at[ph])
        mine.start()
        return copies, mine

    def finish(ph, copies, mine):
        for copy in copies:
            copy.wait_send()
        mine.wait()
        for k in (2, 1, 3, 0):
            for j in range(2):
                origin = 2 * lax.rem(half_member + 4 - k, 4) + j
                slot = 2 * k + j
                if k == 0:
                    if j == 1:
                        continue
                    origin = member + 1 - 2 * odd_member
                    slot = 1 - odd_member
                pltpu.make_async_remote_copy(
                    src_ref=sendbuf.at[ph, origin],
                    dst_ref=out.at[ph, origin],
                    send_sem=a_send.at[ph, slot],
                    recv_sem=a_recv.at[ph, slot],
                    device_id={"member": origin},
                    device_id_type=MESH,
                ).wait_recv()

    project(0)
    for i in range(2, 5):
        weights[i].wait()
        forwards[i].start()
    forwards[1].wait()

    key_i = iota((128, 128), 0)
    pos_i = iota((128, 128), 1)

    def position(index):
        return (
            jnp.bitwise_and(index // 8, 1) * 8 + jnp.bitwise_and(index // 16, 7)
        ) * 8 + jnp.bitwise_and(index, 7)

    natural = onehot(position(key_i) == pos_i)
    crossed = onehot(position(jnp.bitwise_xor(key_i, 64)) == pos_i)
    edge = jnp.logical_or(band == 0, band == BANDS - 1)
    straight = []
    swapped = []
    for h in range(6):
        turned = nt(natural, bias[h // 3, h % 3]).astype(BF16)
        straight.append(nt(turned, natural) * LOG2E)
        swapped.append(nt(turned, crossed) * LOG2E)
    for t in range(3):
        for w in range(2):
            lo, hi = (2 * t, 2 * t + 1) if w == 0 else (2 * t + 1, 2 * t)
            upper = jnp.where(low, straight[lo], swapped[hi])
            lower = jnp.where(low, swapped[lo], straight[hi])
            lower = jnp.concatenate([lower[64:128], lower[0:64]], axis=0)
            first_side = side[0] == 1
            biasl[0, w, t] = jnp.where(first_side, upper, lower)
            second = jnp.where(first_side, lower, upper)
            biasl[1, w, t] = jnp.where(jnp.logical_and(edge, key_i >= 64), -1e9, second)

    attend(0)
    for i in range(2, 5):
        forwards[i].wait()
    heads_in = [wout[h // 3, 32 * (h % 3) : 32 * (h % 3) + 32] for h in (0, 2, 4, 1, 3, 5)]
    wout_t[...] = nt(eye(C), jnp.concatenate(heads_in, axis=0)).astype(BF16)
    for half in range(2):
        wup_t[half * 384 : half * 384 + 384, :] = nt(eye(384), wup[half]).astype(BF16)
    mlp(0)
    first_sent = send(0)
    halos[1].wait()
    halo_rows(1)
    project(1)
    attend(1)
    mlp(1)
    second_sent = send(1)
    finish(0, *first_sent)
    finish(1, *second_sent)


def forecast(off, prior, wqkv, wout, wup, wdown, bias, head):
    vmem = pltpu.VMEM
    dma = pltpu.SemaphoreType.DMA
    hbm = pl.BlockSpec(memory_space=pl.ANY)
    return pl.pallas_call(
        forecast_kernel,
        out_shape=jax.ShapeDtypeStruct((2, MEMBERS, NV, 128), BF16),
        in_specs=[pl.BlockSpec(memory_space=pltpu.SMEM)] + [hbm] * 7,
        out_specs=hbm,
        scratch_shapes=[
            vmem((2, 8, C, 128), BF16),
            vmem((2, 2, 4, C, 128), BF16),
            vmem((2, 3, C, 96), BF16),
            vmem((2, 96, C), BF16),
            vmem((2, C, 384), BF16),
            vmem((2, C, 384), BF16),
            vmem((2, 3, 128, 128), BF16),
            vmem((NV, C), BF16),
            vmem((3, C, C), BF16),
            vmem((C, C), BF16),
            vmem((FF, C), BF16),
            vmem((2, 2, 3, 128, 128), F32),
            vmem((256, 256), BF16),
            vmem((1024, 1024), BF16),
            vmem((2, 16, 8, 16, C), BF16),
            vmem((2, 16, 4, 16, C), BF16),
            vmem((2048, C), BF16),
            vmem((8, C, 256), BF16),
            vmem((8, 2, C, 128), BF16),
            vmem((2, 128, 384), F32),
            vmem((2, 128, 384), BF16),
            vmem((C, 1024), BF16),
            vmem((C, 1024), F32),
            vmem((C, 1024), BF16),
            vmem((FF, 1024), BF16),
            vmem((NV, 1024), BF16),
            vmem((2, MEMBERS, NV, 128), BF16),
            dma((7,)),
            dma((2,)),
            dma((2,)),
            dma((5,)),
            dma((5,)),
            dma((5,)),
            dma((5,)),
            dma((2, MEMBERS)),
            dma((2, MEMBERS)),
            dma((2,)),
        ],
        compiler_params=pltpu.CompilerParams(
            collective_id=0, has_side_effects=True, vmem_limit_bytes=60 * 1024 * 1024
        ),
        cost_estimate=pl.CostEstimate(
            flops=3_000_000_000, bytes_accessed=6_000_000, transcendentals=3_200_000
        ),
        name="forecast",
    )(off, prior, wqkv, wout, wup, wdown, bias, head)


def analysis_kernel(recv, index, count, value, weight, out, xf, vt, ybuf):
    parity = lax.rem(lax.axis_index("band"), 2)
    eye128 = eye(128)
    for ph in range(2):
        base = 4 * (1 - parity) if ph == 0 else 4 * parity
        for m in range(MEMBERS):
            x = nt(eye128, recv[ph, m])
            xf[m, :, pl.ds(base, 4), :, 0:NV] = x.reshape(2, 4, 16, NV)

    lane = iota((128, 128), 1)
    pad = jnp.zeros((128, 112), jnp.int32)
    spread_index = jnp.concatenate([index[0].reshape(128, 16), pad], axis=1)
    idx = jnp.take_along_axis(spread_index, lane // 8, axis=1, mode="promise_in_bounds")
    level = idx >= NV
    inner = jnp.where(level, idx - NV, idx)
    upper = inner >= 128
    inner = jnp.bitwise_and(inner, 127)
    slot_member = jnp.bitwise_and(lane, 7)
    observed = jnp.zeros((128, 128), F32)
    for m in range(MEMBERS):
        picks = []
        for a in range(2):
            for part in range(2):
                x = xf[m, a, :, :, 128 * part : 128 * part + 128].reshape(128, 128)
                picks.append(jnp.take_along_axis(x, inner, axis=1, mode="promise_in_bounds"))
        got = jnp.where(
            level,
            jnp.where(upper, picks[3], picks[2]),
            jnp.where(upper, picks[1], picks[0]),
        )
        observed = jnp.where(slot_member == m, got, observed)
    obs_t = observed.T

    blank = jnp.zeros((128, 96), F32)
    terms = jnp.concatenate(
        [value[0].reshape(128, 16), weight[0].reshape(128, 16), blank], axis=1
    ).T
    counts = count[0].astype(F32).astype(BF16)
    spread = onehot(iota((16, 128), 0) == jnp.bitwise_and(iota((16, 128), 1), 15))
    wide = nn(counts, spread)
    live_count = jnp.sum(
        jnp.where(iota((8, 128), 0) == iota((8, 128), 1) // 16, wide, 0.0), axis=0, keepdims=True
    )

    sub = iota((8, 128), 0)
    rows = [jnp.zeros((8, 128), F32) for _ in range(MEMBERS)]
    right = jnp.zeros((8, 128), F32)
    for k in range(16):
        y = obs_t[8 * k : 8 * k + 8]
        mean = jnp.sum(y, axis=0, keepdims=True) * (1.0 / MEMBERS)
        dev = y - mean
        r = jnp.where(live_count > k, terms[16 + k : 17 + k], 0.0)
        scaled = dev * r
        right = right + scaled * (terms[k : k + 1] - mean)
        for i in range(MEMBERS):
            rows[i] = rows[i] + scaled[i : i + 1] * dev
    for i in range(MEMBERS):
        rows[i] = rows[i] + jnp.where(sub == i, MEMBERS - 1.0, 0.0)
    diagonal = jnp.zeros((8, 128), F32)
    for i in range(MEMBERS):
        diagonal = diagonal + jnp.where(sub == i, rows[i], 0.0)
    trace = jnp.sum(diagonal, axis=0, keepdims=True)
    inverse_trace = 1.0 / trace
    g = [row * inverse_trace for row in rows]

    def product(left, right_mat):
        result = []
        for i in range(MEMBERS):
            total = left[i][0:1] * right_mat[0]
            for j in range(1, MEMBERS):
                total = total + left[i][j : j + 1] * right_mat[j]
            result.append(total)
        return result

    def factor_of(zg):
        return [jnp.where(sub == i, 1.5, 0.0) - 0.5 * zg[i] for i in range(MEMBERS)]

    f = factor_of(g)
    g = product(g, f)
    z = f
    for step in range(1, NEWTON):
        f = factor_of(product(z, g))
        if step < NEWTON - 1:
            g = product(g, f)
        z = product(f, z)

    def apply(mat, vec):
        total = mat[0] * vec[0:1]
        for j in range(1, MEMBERS):
            total = total + mat[j] * vec[j : j + 1]
        return total

    wbar = apply(z, apply(z, right)) * inverse_trace
    scale = math.sqrt(MEMBERS - 1.0) * lax.rsqrt(trace)
    full = [wbar[i : i + 1] + z[i] * scale for i in range(MEMBERS)]
    mean_row = full[0]
    for i in range(1, MEMBERS):
        mean_row = mean_row + full[i]
    shift = (1.0 - mean_row) * (1.0 / MEMBERS)
    low = iota((1, 128), 1) < 64
    for i in range(MEMBERS):
        value_i = full[i] + shift
        turned = pltpu.roll(value_i, 64, 1)
        first = jnp.where(low, value_i, turned)
        second = jnp.where(low, turned, value_i)
        vt[0, i] = jnp.where(parity == 1, first, second)
        vt[1, i] = jnp.where(parity == 1, second, first)

    def update(n, _):
        at = pl.ds(pl.multiple_of(n * 16, 16), 16)
        for ph in range(2):
            x = [recv[ph, i, at, :].astype(F32) for i in range(MEMBERS)]
            for m in range(MEMBERS):
                total = vt[ph, 0, m : m + 1, :] * x[0]
                for i in range(1, MEMBERS):
                    total = total + vt[ph, i, m : m + 1, :] * x[i]
                high = total.astype(BF16)
                ybuf[0, ph, m, at, :] = high
                ybuf[1, ph, m, at, :] = (total - high.astype(F32)).astype(BF16)
        return 0

    lax.fori_loop(0, NV // 16, update, 0)

    for ph in range(2):
        base = 4 * (1 - parity) if ph == 0 else 4 * parity
        for m in range(MEMBERS):
            x = nt(eye128, ybuf[0, ph, m]) + nt(eye128, ybuf[1, ph, m])
            out[m, :, pl.ds(base, 4), :, :] = x.reshape(2, 4, 16, NV)


def analyse(recv, index, count, value, weight):
    return pl.pallas_call(
        analysis_kernel,
        out_shape=jax.ShapeDtypeStruct((MEMBERS, 2, 8, 16, NV), F32),
        scratch_shapes=[
            pltpu.VMEM((MEMBERS, 2, 8, 16, 256), F32),
            pltpu.VMEM((2, MEMBERS, MEMBERS, 128), F32),
            pltpu.VMEM((2, 2, MEMBERS, NV, 128), BF16),
        ],
        compiler_params=pltpu.CompilerParams(vmem_limit_bytes=48 * 1024 * 1024),
        cost_estimate=pl.CostEstimate(
            flops=20_000_000, bytes_accessed=3_000_000, transcendentals=0
        ),
        name="analyse",
    )(recv, index, count, value, weight)


def shards(
    prior_grids,
    w_qkv,
    w_out,
    w_up,
    w_down,
    head_weight,
    pos_bias,
    zonal_offsets,
    obs_index,
    obs_count,
    obs_value,
    obs_weight,
):
    recv = forecast(
        zonal_offsets,
        prior_grids.transpose(0, 1, 2, 4, 3),
        w_qkv.transpose(1, 0, 2),
        w_out,
        w_up,
        w_down.T,
        pos_bias,
        head_weight.T,
    )
    return analyse(recv, obs_index, obs_count, obs_value, obs_weight)


def solution(mesh):
    return jax.shard_map(
        shards,
        mesh=mesh,
        in_specs=(
            P("member", None, "band", None, None),
            P(None, None, "tensor"),
            P("tensor", None),
            P(None, "tensor"),
            P("tensor", None),
            P(),
            P("tensor", None, None),
            P("member"),
            P("tensor", "band", "member", None),
            P("tensor", "band", "member"),
            P("tensor", "band", "member", None),
            P("tensor", "band", "member", None),
        ),
        out_specs=P(None, "tensor", "band", "member", None),
        check_vma=False,
    )
```

```python
import functools
import math

import jax
import jax.numpy as jnp
from jax import lax
from jax.experimental import pallas as pl
from jax.experimental.pallas import tpu as pltpu
from jax.sharding import PartitionSpec as P

F32 = jnp.float32
BF16 = jnp.bfloat16
MESH = pl.DeviceIdType.MESH
C = 192
FF = 768
NV = 160
NEWTON = 8
MEMBERS = 8
BANDS = 16
LOG2E = 1.4426950408889634


def nt(a, b):
    return lax.dot_general(a, b, (((1,), (1,)), ((), ())), preferred_element_type=F32)


def nn(a, b):
    return jnp.dot(a, b, preferred_element_type=F32)


def iota(shape, dim):
    return lax.broadcasted_iota(jnp.int32, shape, dim)


def onehot(cond):
    return jnp.where(cond, 1.0, 0.0).astype(BF16)


def eye(n):
    return onehot(iota((n, n), 0) == iota((n, n), 1))


def gelu(x):
    return 0.5 * x * (1.0 + lax.erf(x * 0.7071067811865476))


def forecast_kernel(
    off_ref,
    prior,
    wqkv_in,
    wout_in,
    wup_in,
    wdown_in,
    bias_in,
    head_in,
    out,
    xown,
    halo,
    wqkv,
    wout,
    wup,
    wdown,
    bias,
    head_t,
    wqkv_t,
    wout_t,
    wup_t,
    biasl,
    perm,
    sendperm,
    nbuf,
    xbuf,
    kbuf,
    vbuf,
    qbuf,
    sbuf,
    pbuf,
    mixbuf,
    onebuf,
    nextbuf,
    actbuf,
    fbuf,
    sendbuf,
    local_sem,
    halo_send,
    halo_recv,
    w_send,
    w_recv,
    f_send,
    f_recv,
    a_send,
    a_recv,
    a_local,
):
    member = lax.axis_index("member")
    band = lax.axis_index("band")
    tensor = lax.axis_index("tensor")
    parity = lax.rem(band, 2)
    other = 1 - tensor
    sibling = band + 1 - 2 * parity
    far = lax.rem(band + 2 * parity - 1 + BANDS, BANDS)
    xband = lax.rem(band + BANDS // 2, BANDS)
    side = (1 - parity, parity)

    barrier = pltpu.get_barrier_semaphore()
    pl.semaphore_signal(barrier, inc=1, device_id={"band": sibling}, device_id_type=MESH)
    pl.semaphore_signal(barrier, inc=1, device_id={"band": far}, device_id_type=MESH)
    pl.semaphore_signal(
        barrier, inc=1, device_id={"band": xband, "tensor": other}, device_id_type=MESH
    )
    for k in range(1, MEMBERS):
        pl.semaphore_signal(
            barrier,
            inc=1,
            device_id={"member": lax.rem(member + k, MEMBERS)},
            device_id_type=MESH,
        )

    def part(ref, i, half, c):
        if i == 0:
            return ref.at[half, :, pl.ds(c * 96, 96)]
        if i == 1:
            return ref.at[half, :, pl.ds(c * 64, 64)]
        if i == 2:
            return ref.at[half, pl.ds(c * 48, 48)]
        return ref.at[half, pl.ds(c * 96, 96)]

    def src_part(ref, i, c):
        if i == 0:
            return ref.at[:, pl.ds(c * 96, 96)]
        if i == 1:
            return ref.at[:, pl.ds(c * 64, 64)]
        if i == 2:
            return ref.at[pl.ds(c * 48, 48)]
        return ref.at[pl.ds(c * 96, 96)]

    sources = (wqkv_in, bias_in, wout_in, wup_in, wdown_in)
    targets = (wqkv, bias, wout, wup, wdown)

    own_x = pltpu.make_async_copy(
        prior.at[0, pl.ds(2 * tensor, 2)], xown, local_sem.at[0]
    )
    own_x.start()
    locals_ = []
    for i in range(5):
        locals_.append(
            pltpu.make_async_copy(sources[i], targets[i].at[tensor], local_sem.at[1 + i])
        )
    locals_.append(pltpu.make_async_copy(head_in, head_t, local_sem.at[6]))
    for copy in locals_:
        copy.start()

    offset = off_ref[0]
    row_i = iota((256, 256), 0)
    col_i = iota((256, 256), 1)
    place = jnp.bitwise_and((row_i // 16) * 8 + jnp.bitwise_and(row_i, 7) + offset, 127)
    want = jnp.bitwise_and(row_i // 8, 1) * 128 + place
    perm[...] = onehot(want == col_i)

    def build_send(i, _):
        rows = iota((64, 1024), 0)
        cols = iota((64, 1024), 1)
        level = jnp.bitwise_and(rows // 8, 1)
        row = rows // 16
        where = jnp.bitwise_and(i * 8 + jnp.bitwise_and(rows, 7) + offset, 127)
        target = (where // 16) * 128 + level * 64 + row * 16 + jnp.bitwise_and(where, 15)
        sendperm[pl.ds(pl.multiple_of(i * 64, 64), 64), :] = onehot(target == cols)
        return 0

    pl.semaphore_wait(barrier, 3 + MEMBERS - 1)

    halos = []
    for ph, peer in ((0, sibling), (1, far)):
        halos.append(
            pltpu.make_async_remote_copy(
                src_ref=prior.at[0, pl.ds(2 * tensor, 2), pl.ds(4 * side[ph], 4)],
                dst_ref=halo.at[ph],
                send_sem=halo_send.at[ph],
                recv_sem=halo_recv.at[ph],
                device_id={"band": peer},
                device_id_type=MESH,
            )
        )
    weights = []
    forwards = []
    for i in range(5):
        weights.append(
            pltpu.make_async_remote_copy(
                src_ref=src_part(sources[i], i, parity),
                dst_ref=part(targets[i], i, tensor, parity),
                send_sem=w_send.at[i],
                recv_sem=w_recv.at[i],
                device_id={"band": xband, "tensor": other},
                device_id_type=MESH,
            )
        )
        piece = part(targets[i], i, other, parity)
        forwards.append(
            pltpu.make_async_remote_copy(
                src_ref=piece,
                dst_ref=piece,
                send_sem=f_send.at[i],
                recv_sem=f_recv.at[i],
                device_id={"band": sibling},
                device_id_type=MESH,
            )
        )
    weights[0].start()
    halos[0].start()
    weights[1].start()
    halos[1].start()
    for i in range(2, 5):
        weights[i].start()

    def prepare(block, ph, slot, keep):
        tokens = block.astype(F32)
        mean = jnp.sum(tokens, axis=0, keepdims=True) * (1.0 / C)
        center = tokens - mean
        spread = jnp.sum(center * center, axis=0, keepdims=True) * (1.0 / C)
        normed = (center * lax.rsqrt(spread + 1e-05)).astype(BF16)
        nbuf[ph, :, slot] = nt(perm[...], normed).astype(BF16).reshape(16, 16, C)
        if keep:
            xbuf[ph, :, slot] = nt(perm[...], block).astype(BF16).reshape(16, 16, C)

    own_x.wait()
    for ph in range(2):
        for r in range(4):
            row = 4 * side[ph] + r
            prepare(jnp.concatenate([xown[0, row], xown[1, row]], axis=1), ph, r, True)

    def halo_rows(ph):
        for r in range(4):
            prepare(jnp.concatenate([halo[ph, 0, r], halo[ph, 1, r]], axis=1), ph, 4 + r, False)

    lax.fori_loop(0, 16, build_send, 0)
    for copy in locals_:
        copy.wait()
    weights[0].wait()
    forwards[0].start()
    halos[0].wait()
    halo_rows(0)
    weights[1].wait()
    forwards[1].start()
    forwards[0].wait()

    for half in range(2):
        for i in range(3):
            turned = nt(eye(96), wqkv[half, i]).astype(BF16)
            if i > 0:
                wqkv_t[i, half * 96 : half * 96 + 96] = turned
                continue
            for n in range(3):
                h = 3 * half + n
                to = (h // 2) * 32 + (h % 2) * 96
                wqkv_t[0, to : to + 32] = turned[32 * n : 32 * n + 32]

    lane = iota((1, 128), 1)
    low = lane < 64

    def project(ph):
        wk, wv = wqkv_t[1], wqkv_t[2]
        wq_even, wq_odd = wqkv_t[0, 0:96], wqkv_t[0, 96:192]
        wide_low = jnp.bitwise_and(iota((1, 256), 1), 127) < 64
        for j in range(4):
            tokens = nbuf[ph, 4 * j : 4 * j + 4].reshape(512, C)
            own = nbuf[ph, 4 * j : 4 * j + 4, 0:4].reshape(4, 64, C)
            swapped = jnp.concatenate([own[1], own[0], own[3], own[2]], axis=0)
            kbuf[512 * j : 512 * j + 512, :] = nt(tokens, wk).astype(BF16)
            v = nt(wv, tokens).astype(BF16)
            q = jnp.concatenate([nt(wq_even, own.reshape(256, C)), nt(wq_odd, swapped)], axis=0)
            lows = jnp.where(wide_low, q, 0.0).astype(BF16)
            highs = jnp.where(wide_low, 0.0, q).astype(BF16)
            for i in range(2):
                vbuf[2 * j + i] = v[:, 256 * i : 256 * i + 256]
                qbuf[2 * j + i, 0] = lows[:, 128 * i : 128 * i + 128]
                qbuf[2 * j + i, 1] = highs[:, 128 * i : 128 * i + 128]

    zero64 = jnp.zeros((64, 128), BF16)
    ones16 = jnp.ones((16, 128), BF16)

    def attend(ph, begin, end):
        def step(i, _):
            j = jnp.clip(i - 2, 0, 7)
            results = []
            for w in range(2):
                result = []
                for t in range(3):
                    left = jnp.concatenate(
                        [vbuf[j, 64 * t : 64 * t + 64, 128 * w : 128 * w + 128], ones16], axis=0
                    )
                    result.append(nn(left, pbuf[w, :, 128 * t : 128 * t + 128]))
                results.append(result)
            where = pl.ds(pl.multiple_of(128 * j, 128), 128)
            for t in range(3):
                a, b = results[0][t], results[1][t]
                even = jnp.where(low, a[0:32], b[0:32])
                even = even * (1.0 / jnp.where(low, a[64:65], b[64:65]))
                odd = jnp.where(low, b[32:64], a[32:64])
                odd = odd * (1.0 / jnp.where(low, b[64:65], a[64:65]))
                mixbuf[32 * t : 32 * t + 32, where] = even.astype(BF16)
                mixbuf[96 + 32 * t : 128 + 32 * t, where] = odd.astype(BF16)

            for w in range(2):
                for t in range(3):
                    s = sbuf[w, :, 128 * t : 128 * t + 128] * (LOG2E * 32**-0.5)
                    s = s + biasl[ph, w, t]
                    s = s - jnp.max(s, axis=0, keepdims=True)
                    pbuf[w, :, 128 * t : 128 * t + 128] = jnp.exp2(s).astype(BF16)

            j = jnp.minimum(i, 7)
            for w in range(2):
                columns = []
                for t in range(3):
                    pieces = [zero64] * 3
                    pieces[t] = jnp.concatenate(
                        [
                            qbuf[j, w, 32 * t : 32 * t + 32],
                            qbuf[j, 1 - w, 96 + 32 * t : 128 + 32 * t],
                        ],
                        axis=0,
                    )
                    columns.append(jnp.concatenate(pieces, axis=0))
                start = pl.multiple_of(256 * j + 128 * w, 128)
                sbuf[w] = nn(kbuf[pl.ds(start, 128), :], jnp.concatenate(columns, axis=1))
            return 0

        lax.fori_loop(begin, end, step, 0)

    def mlp(ph):
        def first(j):
            cols = slice(256 * j, 256 * j + 256)
            prior_t = nt(eye(C), xbuf[ph, 4 * j : 4 * j + 4].reshape(256, C))
            odd = mixbuf[96:192, cols].astype(F32)
            odd = jnp.concatenate(
                [pltpu.roll(odd[:, 0:128], 64, 1), pltpu.roll(odd[:, 128:256], 64, 1)], axis=1
            ).astype(BF16)
            mixed = jnp.concatenate([mixbuf[0:96, cols], odd], axis=0)
            one = prior_t + nn(wout_t[...], mixed)
            onebuf[:, cols] = one
            mean = jnp.sum(one, axis=0, keepdims=True) * (1.0 / C)
            center = one - mean
            spread = jnp.sum(center * center, axis=0, keepdims=True) * (1.0 / C)
            nextbuf[:, cols] = (center * lax.rsqrt(spread + 1e-05)).astype(BF16)

        def second(j):
            cols = slice(256 * j, 256 * j + 256)
            actbuf[:, cols] = gelu(nn(wup_t[...], nextbuf[:, cols])).astype(BF16)

        def third(j):
            cols = slice(256 * j, 256 * j + 256)
            raised = nn(wdown[0], actbuf[0:384, cols]) + nn(wdown[1], actbuf[384:768, cols])
            two = (onebuf[:, cols] + raised).astype(BF16)
            fbuf[:, cols] = nn(head_t[...], two).astype(BF16)

        for j in range(6):
            if 0 <= j - 2 < 4:
                if ph == 0 and j == 2:
                    forwards[4].wait()
                third(j - 2)
            if 0 <= j - 1 < 4:
                second(j - 1)
            if j < 4:
                first(j)

    half_member = member // 2
    odd_member = lax.rem(member, 2)

    def send(ph):
        copies = []
        for k in (2, 1, 3, 0):
            pair = lax.rem(half_member + k, 4)
            cols = pl.ds(pl.multiple_of(256 * pair, 256), 256)
            sent = nn(fbuf[...], sendperm[:, cols]).astype(BF16)
            for j in range(2):
                sendbuf[ph, 2 * pair + j] = sent[:, 128 * j : 128 * j + 128]
            for j in range(2):
                to = 2 * pair + j
                if k == 0:
                    if j == 1:
                        continue
                    to = member + 1 - 2 * odd_member
                copy = pltpu.make_async_remote_copy(
                    src_ref=sendbuf.at[ph, to],
                    dst_ref=out.at[ph, member],
                    send_sem=a_send.at[ph, 2 * k + j],
                    recv_sem=a_recv.at[ph, 2 * k + odd_member],
                    device_id={"member": to},
                    device_id_type=MESH,
                )
                copy.start()
                copies.append(copy)
        mine = pltpu.make_async_copy(sendbuf.at[ph, member], out.at[ph, member], a_local.at[ph])
        mine.start()
        return copies, mine

    def finish(ph, copies, mine):
        for copy in copies:
            copy.wait_send()
        mine.wait()
        for k in (2, 1, 3, 0):
            for j in range(2):
                origin = 2 * lax.rem(half_member + 4 - k, 4) + j
                slot = 2 * k + j
                if k == 0:
                    if j == 1:
                        continue
                    origin = member + 1 - 2 * odd_member
                    slot = 1 - odd_member
                pltpu.make_async_remote_copy(
                    src_ref=sendbuf.at[ph, origin],
                    dst_ref=out.at[ph, origin],
                    send_sem=a_send.at[ph, slot],
                    recv_sem=a_recv.at[ph, slot],
                    device_id={"member": origin},
                    device_id_type=MESH,
                ).wait_recv()

    project(0)
    for i in range(2, 5):
        weights[i].wait()
        forwards[i].start()
    forwards[1].wait()

    key_i = iota((128, 128), 0)
    pos_i = iota((128, 128), 1)

    def position(index):
        return (
            jnp.bitwise_and(index // 8, 1) * 8 + jnp.bitwise_and(index // 16, 7)
        ) * 8 + jnp.bitwise_and(index, 7)

    natural = onehot(position(key_i) == pos_i)
    crossed = onehot(position(jnp.bitwise_xor(key_i, 64)) == pos_i)
    edge = jnp.logical_or(band == 0, band == BANDS - 1)
    straight = []
    swapped = []
    for h in range(6):
        turned = nt(natural, bias[h // 3, h % 3]).astype(BF16)
        straight.append(nt(turned, natural) * LOG2E)
        swapped.append(nt(turned, crossed) * LOG2E)
    for t in range(3):
        for w in range(2):
            lo, hi = (2 * t, 2 * t + 1) if w == 0 else (2 * t + 1, 2 * t)
            upper = jnp.where(low, straight[lo], swapped[hi])
            lower = jnp.where(low, swapped[lo], straight[hi])
            lower = jnp.concatenate([lower[64:128], lower[0:64]], axis=0)
            first_side = side[0] == 1
            biasl[0, w, t] = jnp.where(first_side, upper, lower)
            second = jnp.where(first_side, lower, upper)
            biasl[1, w, t] = jnp.where(jnp.logical_and(edge, key_i >= 64), -1e9, second)

    attend(0, 0, 10)
    forwards[2].wait()
    heads_in = [wout[h // 3, 32 * (h % 3) : 32 * (h % 3) + 32] for h in (0, 2, 4, 1, 3, 5)]
    wout_t[...] = nt(eye(C), jnp.concatenate(heads_in, axis=0)).astype(BF16)
    forwards[3].wait()
    for half in range(2):
        wup_t[half * 384 : half * 384 + 384, :] = nt(eye(384), wup[half]).astype(BF16)
    mlp(0)
    first_sent = send(0)
    halos[1].wait()
    halo_rows(1)
    project(1)
    attend(1, 0, 10)
    mlp(1)
    second_sent = send(1)
    finish(0, *first_sent)
    finish(1, *second_sent)


def forecast(off, prior, wqkv, wout, wup, wdown, bias, head):
    vmem = pltpu.VMEM
    dma = pltpu.SemaphoreType.DMA
    hbm = pl.BlockSpec(memory_space=pl.ANY)
    return pl.pallas_call(
        forecast_kernel,
        out_shape=jax.ShapeDtypeStruct((2, MEMBERS, NV, 128), BF16),
        in_specs=[pl.BlockSpec(memory_space=pltpu.SMEM)] + [hbm] * 7,
        out_specs=pl.BlockSpec(memory_space=pl.ANY),
        scratch_shapes=[
            vmem((2, 8, C, 128), BF16),
            vmem((2, 2, 4, C, 128), BF16),
            vmem((2, 3, C, 96), BF16),
            vmem((2, 96, C), BF16),
            vmem((2, C, 384), BF16),
            vmem((2, C, 384), BF16),
            vmem((2, 3, 128, 128), BF16),
            vmem((NV, C), BF16),
            vmem((3, C, C), BF16),
            vmem((C, C), BF16),
            vmem((FF, C), BF16),
            vmem((2, 2, 3, 128, 128), F32),
            vmem((256, 256), BF16),
            vmem((1024, 1024), BF16),
            vmem((2, 16, 8, 16, C), BF16),
            vmem((2, 16, 4, 16, C), BF16),
            vmem((2048, C), BF16),
            vmem((8, C, 256), BF16),
            vmem((8, 2, C, 128), BF16),
            vmem((2, 128, 384), F32),
            vmem((2, 128, 384), BF16),
            vmem((C, 1024), BF16),
            vmem((C, 1024), F32),
            vmem((C, 1024), BF16),
            vmem((FF, 1024), BF16),
            vmem((NV, 1024), BF16),
            vmem((2, MEMBERS, NV, 128), BF16),
            dma((7,)),
            dma((2,)),
            dma((2,)),
            dma((5,)),
            dma((5,)),
            dma((5,)),
            dma((5,)),
            dma((2, MEMBERS)),
            dma((2, MEMBERS)),
            dma((2,)),
        ],
        compiler_params=pltpu.CompilerParams(
            collective_id=0, has_side_effects=True, vmem_limit_bytes=60 * 1024 * 1024
        ),
        cost_estimate=pl.CostEstimate(
            flops=3_000_000_000, bytes_accessed=6_000_000, transcendentals=3_200_000
        ),
        name="forecast",
    )(off, prior, wqkv, wout, wup, wdown, bias, head)


def analysis_kernel(
    arrived,
    index_in,
    count_in,
    value_in,
    weight_in,
    out,
    recv,
    index,
    count,
    value,
    weight,
    in_sem,
    xf,
    vt,
    ybuf,
    obuf,
    work,
    scaled_ref,
    out_sem,
):
    parity = lax.rem(lax.axis_index("band"), 2)
    loads = []
    for ph in range(2):
        load = pltpu.make_async_copy(arrived.at[ph], recv.at[ph], in_sem.at[ph])
        load.start()
        loads.append(load)
    observations = []
    for n, (src, dst) in enumerate(
        ((index_in, index), (count_in, count), (value_in, value), (weight_in, weight))
    ):
        load = pltpu.make_async_copy(src, dst, in_sem.at[2 + n])
        load.start()
        observations.append(load)
    eye128 = eye(128)
    fold = onehot(jnp.bitwise_and(iota((64, 128), 1), 63) == iota((64, 128), 0))
    low_level = onehot(iota((1, 128), 1) < 64)
    high_level = onehot(iota((1, 128), 1) >= 64)
    for ph in range(2):
        base = 4 * (1 - parity) if ph == 0 else 4 * parity
        loads[ph].wait()
        for m in range(MEMBERS):
            block = recv[ph, m]
            both = jnp.concatenate([block * low_level, block * high_level], axis=0)
            xf[m, pl.ds(base * 16, 64), 0 : 2 * NV] = nt(fold, both)

    for load in observations:
        load.wait()
    lane = iota((128, 128), 1)
    pad = jnp.zeros((128, 112), jnp.int32)
    spread_index = jnp.concatenate([index[0].reshape(128, 16), pad], axis=1)
    idx = jnp.take_along_axis(spread_index, lane // 8, axis=1, mode="promise_in_bounds")
    tile = idx // 128
    inner = jnp.bitwise_and(idx, 127)
    slot_member = jnp.bitwise_and(lane, 7)
    observed = jnp.zeros((128, 128), F32)
    for m in range(MEMBERS):
        picks = []
        for part in range(3):
            x = xf[m, :, 128 * part : 128 * part + 128]
            picks.append(jnp.take_along_axis(x, inner, axis=1, mode="promise_in_bounds"))
        got = jnp.where(tile == 0, picks[0], jnp.where(tile == 1, picks[1], picks[2]))
        observed = jnp.where(slot_member == m, got, observed)
    obs_t = observed.T

    blank = jnp.zeros((128, 96), F32)
    terms = jnp.concatenate(
        [value[0].reshape(128, 16), weight[0].reshape(128, 16), blank], axis=1
    ).T
    counts = count[0].astype(F32).astype(BF16)
    spread = onehot(iota((16, 128), 0) == jnp.bitwise_and(iota((16, 128), 1), 15))
    wide = nn(counts, spread)
    live_count = jnp.sum(
        jnp.where(iota((8, 128), 0) == iota((8, 128), 1) // 16, wide, 0.0), axis=0, keepdims=True
    )

    sub = iota((8, 128), 0)
    rows = [jnp.zeros((8, 128), F32) for _ in range(MEMBERS)]
    right = jnp.zeros((8, 128), F32)
    devs = []
    for k in range(16):
        y = obs_t[8 * k : 8 * k + 8]
        mean = jnp.sum(y, axis=0, keepdims=True) * (1.0 / MEMBERS)
        dev = y - mean
        devs.append(dev)
        r = jnp.where(live_count > k, terms[16 + k : 17 + k], 0.0)
        scaled = dev * r
        right = right + scaled * (terms[k : k + 1] - mean)
        scaled_ref[k] = scaled
    for k in range(16):
        for i in range(MEMBERS):
            rows[i] = rows[i] + scaled_ref[k, i : i + 1, :] * devs[k]
    for i in range(MEMBERS):
        rows[i] = rows[i] + jnp.where(sub == i, MEMBERS - 1.0, 0.0)
    diagonal = jnp.zeros((8, 128), F32)
    for i in range(MEMBERS):
        diagonal = diagonal + jnp.where(sub == i, rows[i], 0.0)
    trace = jnp.sum(diagonal, axis=0, keepdims=True)
    inverse_trace = 1.0 / trace
    g = [row * inverse_trace for row in rows]

    def product(slot, right_mat):
        result = []
        for i in range(MEMBERS):
            terms_ = [work[slot, i, j : j + 1, :] * right_mat[j] for j in range(MEMBERS)]
            while len(terms_) > 1:
                terms_ = [terms_[n] + terms_[n + 1] for n in range(0, len(terms_), 2)]
            result.append(terms_[0])
        return result

    def keep(slot, mat):
        for i in range(MEMBERS):
            work[slot, i] = mat[i]

    def factor_of(zg):
        return [jnp.where(sub == i, 1.5, 0.0) - 0.5 * zg[i] for i in range(MEMBERS)]

    f = factor_of(g)
    keep(0, g)
    g = product(0, f)
    z = f
    keep(1, z)
    for step in range(1, NEWTON):
        f = factor_of(product(1, g))
        keep(2, f)
        if step < NEWTON - 1:
            keep(0, g)
            g = product(0, f)
        z = product(2, z)
        keep(1, z)

    def apply(mat, vec):
        total = mat[0] * vec[0:1]
        for j in range(1, MEMBERS):
            total = total + mat[j] * vec[j : j + 1]
        return total

    wbar = apply(z, apply(z, right)) * inverse_trace
    scale = math.sqrt(MEMBERS - 1.0) * lax.rsqrt(trace)
    full = [wbar[i : i + 1] + z[i] * scale for i in range(MEMBERS)]
    mean_row = full[0]
    for i in range(1, MEMBERS):
        mean_row = mean_row + full[i]
    shift = (1.0 - mean_row) * (1.0 / MEMBERS)
    low = iota((1, 128), 1) < 64
    for i in range(MEMBERS):
        value_i = full[i] + shift
        turned = pltpu.roll(value_i, 64, 1)
        first = jnp.where(low, value_i, turned)
        second = jnp.where(low, turned, value_i)
        vt[0, i] = jnp.where(parity == 1, first, second)
        vt[1, i] = jnp.where(parity == 1, second, first)

    def update(n, _):
        at = pl.ds(pl.multiple_of(n * 16, 16), 16)
        for ph in range(2):
            x = [recv[ph, i, at, :].astype(F32) for i in range(MEMBERS)]
            for m in range(MEMBERS):
                total = vt[ph, 0, m : m + 1, :] * x[0]
                for i in range(1, MEMBERS):
                    total = total + vt[ph, i, m : m + 1, :] * x[i]
                ybuf[ph, m, at, :] = total.astype(BF16)
        return 0

    lax.fori_loop(0, NV // 16, update, 0, unroll=True)

    copies = []
    for m in range(MEMBERS):
        for ph in range(2):
            base = 4 * (1 - parity) if ph == 0 else 4 * parity
            x = nt(eye128, ybuf[ph, m])
            obuf[m, :, pl.ds(base, 4), :, :] = x.reshape(2, 4, 16, NV)
        copy = pltpu.make_async_copy(obuf.at[m], out.at[m], out_sem.at[m])
        copy.start()
        copies.append(copy)
    for copy in copies:
        copy.wait()


def analyse(recv, index, count, value, weight):
    return pl.pallas_call(
        analysis_kernel,
        out_shape=jax.ShapeDtypeStruct((MEMBERS, 2, 8, 16, NV), F32),
        out_specs=pl.BlockSpec(memory_space=pl.ANY),
        in_specs=[pl.BlockSpec(memory_space=pl.ANY)] * 5,
        scratch_shapes=[
            pltpu.VMEM((2, MEMBERS, NV, 128), BF16),
            pltpu.VMEM((1, 8, 16, 16), jnp.int32),
            pltpu.VMEM((1, 8, 16), jnp.int32),
            pltpu.VMEM((1, 8, 16, 16), F32),
            pltpu.VMEM((1, 8, 16, 16), F32),
            pltpu.SemaphoreType.DMA((6,)),
            pltpu.VMEM((MEMBERS, 128, 384), F32),
            pltpu.VMEM((2, MEMBERS, MEMBERS, 128), F32),
            pltpu.VMEM((2, MEMBERS, NV, 128), BF16),
            pltpu.VMEM((MEMBERS, 2, 8, 16, NV), F32),
            pltpu.VMEM((3, MEMBERS, MEMBERS, 128), F32),
            pltpu.VMEM((16, MEMBERS, 128), F32),
            pltpu.SemaphoreType.DMA((MEMBERS,)),
        ],
        compiler_params=pltpu.CompilerParams(vmem_limit_bytes=60 * 1024 * 1024),
        cost_estimate=pl.CostEstimate(
            flops=20_000_000, bytes_accessed=3_000_000, transcendentals=0
        ),
        name="analyse",
    )(recv, index, count, value, weight)


def shards(
    prior_grids,
    w_qkv,
    w_out,
    w_up,
    w_down,
    head_weight,
    pos_bias,
    zonal_offsets,
    obs_index,
    obs_count,
    obs_value,
    obs_weight,
):
    recv = forecast(
        zonal_offsets,
        prior_grids.transpose(0, 1, 2, 4, 3),
        w_qkv.transpose(1, 0, 2),
        w_out,
        w_up,
        w_down.T,
        pos_bias,
        head_weight.T,
    )
    return analyse(recv, obs_index, obs_count, obs_value, obs_weight)


def solution(mesh):
    return jax.shard_map(
        shards,
        mesh=mesh,
        in_specs=(
            P("member", None, "band", None, None),
            P(None, None, "tensor"),
            P("tensor", None),
            P(None, "tensor"),
            P("tensor", None),
            P(),
            P("tensor", None, None),
            P("member"),
            P("tensor", "band", "member", None),
            P("tensor", "band", "member"),
            P("tensor", "band", "member", None),
            P("tensor", "band", "member", None),
        ),
        out_specs=P(None, "tensor", "band", "member", None),
        check_vma=False,
    )
```

```python
import functools
import math

import jax
import jax.numpy as jnp
from jax import lax
from jax.experimental import pallas as pl
from jax.experimental.pallas import tpu as pltpu
from jax.sharding import PartitionSpec as P

F32 = jnp.float32
BF16 = jnp.bfloat16
MESH = pl.DeviceIdType.MESH
C = 192
FF = 768
NV = 160
NEWTON = 8
MEMBERS = 8
BANDS = 16
LOG2E = 1.4426950408889634


def nt(a, b):
    return lax.dot_general(a, b, (((1,), (1,)), ((), ())), preferred_element_type=F32)


def nn(a, b):
    return jnp.dot(a, b, preferred_element_type=F32)


def iota(shape, dim):
    return lax.broadcasted_iota(jnp.int32, shape, dim)


def onehot(cond):
    return jnp.where(cond, 1.0, 0.0).astype(BF16)


def eye(n):
    return onehot(iota((n, n), 0) == iota((n, n), 1))


def gelu(x):
    return 0.5 * x * (1.0 + lax.erf(x * 0.7071067811865476))


def forecast_kernel(
    off_ref,
    prior,
    wqkv_in,
    wout_in,
    wup_in,
    wdown_in,
    bias_in,
    head_in,
    out,
    xown,
    halo,
    wqkv,
    wout,
    wup,
    wdown,
    bias,
    head_t,
    wqkv_t,
    wout_t,
    wup_t,
    biasl,
    perm,
    sendperm,
    nbuf,
    xbuf,
    kbuf,
    vbuf,
    qbuf,
    sbuf,
    pbuf,
    mixbuf,
    onebuf,
    nextbuf,
    actbuf,
    fbuf,
    sendbuf,
    local_sem,
    halo_send,
    halo_recv,
    w_send,
    w_recv,
    f_send,
    f_recv,
    a_send,
    a_recv,
    a_local,
):
    member = lax.axis_index("member")
    band = lax.axis_index("band")
    tensor = lax.axis_index("tensor")
    parity = lax.rem(band, 2)
    other = 1 - tensor
    sibling = band + 1 - 2 * parity
    far = lax.rem(band + 2 * parity - 1 + BANDS, BANDS)
    xband = lax.rem(band + BANDS // 2, BANDS)
    side = (1 - parity, parity)

    barrier = pltpu.get_barrier_semaphore()
    pl.semaphore_signal(barrier, inc=1, device_id={"band": sibling}, device_id_type=MESH)
    pl.semaphore_signal(barrier, inc=1, device_id={"band": far}, device_id_type=MESH)
    pl.semaphore_signal(
        barrier, inc=1, device_id={"band": xband, "tensor": other}, device_id_type=MESH
    )
    for k in range(1, MEMBERS):
        pl.semaphore_signal(
            barrier,
            inc=1,
            device_id={"member": lax.rem(member + k, MEMBERS)},
            device_id_type=MESH,
        )

    def part(ref, i, half, c):
        if i == 0:
            return ref.at[half, :, pl.ds(c * 96, 96)]
        if i == 1:
            return ref.at[half, :, pl.ds(c * 64, 64)]
        if i == 2:
            return ref.at[half, pl.ds(c * 48, 48)]
        return ref.at[half, pl.ds(c * 96, 96)]

    def src_part(ref, i, c):
        if i == 0:
            return ref.at[:, pl.ds(c * 96, 96)]
        if i == 1:
            return ref.at[:, pl.ds(c * 64, 64)]
        if i == 2:
            return ref.at[pl.ds(c * 48, 48)]
        return ref.at[pl.ds(c * 96, 96)]

    sources = (wqkv_in, bias_in, wout_in, wup_in, wdown_in)
    targets = (wqkv, bias, wout, wup, wdown)

    own_x = pltpu.make_async_copy(
        prior.at[0, pl.ds(2 * tensor, 2)], xown, local_sem.at[0]
    )
    own_x.start()
    locals_ = []
    for i in range(5):
        locals_.append(
            pltpu.make_async_copy(sources[i], targets[i].at[tensor], local_sem.at[1 + i])
        )
    locals_.append(pltpu.make_async_copy(head_in, head_t, local_sem.at[6]))
    for copy in locals_:
        copy.start()

    offset = off_ref[0]
    row_i = iota((256, 256), 0)
    col_i = iota((256, 256), 1)
    place = jnp.bitwise_and((row_i // 16) * 8 + jnp.bitwise_and(row_i, 7) + offset, 127)
    want = jnp.bitwise_and(row_i // 8, 1) * 128 + place
    perm[...] = onehot(want == col_i)

    def build_send(i, _):
        rows = iota((64, 1024), 0)
        cols = iota((64, 1024), 1)
        level = jnp.bitwise_and(rows // 8, 1)
        row = rows // 16
        where = jnp.bitwise_and(i * 8 + jnp.bitwise_and(rows, 7) + offset, 127)
        target = (where // 16) * 128 + level * 64 + row * 16 + jnp.bitwise_and(where, 15)
        sendperm[pl.ds(pl.multiple_of(i * 64, 64), 64), :] = onehot(target == cols)
        return 0

    pl.semaphore_wait(barrier, 3 + MEMBERS - 1)

    halos = []
    for ph, peer in ((0, sibling), (1, far)):
        halos.append(
            pltpu.make_async_remote_copy(
                src_ref=prior.at[0, pl.ds(2 * tensor, 2), pl.ds(4 * side[ph], 4)],
                dst_ref=halo.at[ph],
                send_sem=halo_send.at[ph],
                recv_sem=halo_recv.at[ph],
                device_id={"band": peer},
                device_id_type=MESH,
            )
        )
    weights = []
    forwards = []
    for i in range(5):
        weights.append(
            pltpu.make_async_remote_copy(
                src_ref=src_part(sources[i], i, parity),
                dst_ref=part(targets[i], i, tensor, parity),
                send_sem=w_send.at[i],
                recv_sem=w_recv.at[i],
                device_id={"band": xband, "tensor": other},
                device_id_type=MESH,
            )
        )
        piece = part(targets[i], i, other, parity)
        forwards.append(
            pltpu.make_async_remote_copy(
                src_ref=piece,
                dst_ref=piece,
                send_sem=f_send.at[i],
                recv_sem=f_recv.at[i],
                device_id={"band": sibling},
                device_id_type=MESH,
            )
        )
    weights[0].start()
    halos[0].start()
    weights[1].start()

    def prepare(block, ph, slot, keep):
        tokens = block.astype(F32)
        mean = jnp.sum(tokens, axis=0, keepdims=True) * (1.0 / C)
        center = tokens - mean
        spread = jnp.sum(center * center, axis=0, keepdims=True) * (1.0 / C)
        normed = (center * lax.rsqrt(spread + 1e-05)).astype(BF16)
        nbuf[ph, :, slot] = nt(perm[...], normed).astype(BF16).reshape(16, 16, C)
        if keep:
            xbuf[ph, :, slot] = nt(perm[...], block).astype(BF16).reshape(16, 16, C)

    own_x.wait()
    for ph in range(2):
        for r in range(4):
            row = 4 * side[ph] + r
            prepare(jnp.concatenate([xown[0, row], xown[1, row]], axis=1), ph, r, True)

    def halo_rows(ph):
        for r in range(4):
            prepare(jnp.concatenate([halo[ph, 0, r], halo[ph, 1, r]], axis=1), ph, 4 + r, False)

    for i in range(2, 5):
        weights[i].start()
    halos[1].start()
    lax.fori_loop(0, 16, build_send, 0)
    for copy in locals_:
        copy.wait()
    weights[0].wait()
    forwards[0].start()
    halos[0].wait()
    halo_rows(0)
    weights[1].wait()
    forwards[1].start()
    forwards[0].wait()

    for half in range(2):
        for i in range(3):
            turned = nt(eye(96), wqkv[half, i]).astype(BF16)
            if i > 0:
                wqkv_t[i, half * 96 : half * 96 + 96] = turned
                continue
            for n in range(3):
                h = 3 * half + n
                to = (h // 2) * 32 + (h % 2) * 96
                wqkv_t[0, to : to + 32] = turned[32 * n : 32 * n + 32]

    lane = iota((1, 128), 1)
    low = lane < 64

    def project(ph):
        wk, wv = wqkv_t[1], wqkv_t[2]
        wq_even, wq_odd = wqkv_t[0, 0:96], wqkv_t[0, 96:192]
        wide_low = jnp.bitwise_and(iota((1, 256), 1), 127) < 64
        for j in range(4):
            tokens = nbuf[ph, 4 * j : 4 * j + 4].reshape(512, C)
            own = nbuf[ph, 4 * j : 4 * j + 4, 0:4].reshape(4, 64, C)
            swapped = jnp.concatenate([own[1], own[0], own[3], own[2]], axis=0)
            kbuf[512 * j : 512 * j + 512, :] = nt(tokens, wk).astype(BF16)
            v = nt(wv, tokens).astype(BF16)
            q = jnp.concatenate([nt(wq_even, own.reshape(256, C)), nt(wq_odd, swapped)], axis=0)
            lows = jnp.where(wide_low, q, 0.0).astype(BF16)
            highs = jnp.where(wide_low, 0.0, q).astype(BF16)
            for i in range(2):
                vbuf[2 * j + i] = v[:, 256 * i : 256 * i + 256]
                qbuf[2 * j + i, 0] = lows[:, 128 * i : 128 * i + 128]
                qbuf[2 * j + i, 1] = highs[:, 128 * i : 128 * i + 128]

    zero64 = jnp.zeros((64, 128), BF16)
    ones16 = jnp.ones((16, 128), BF16)

    def attend(ph, begin, end):
        def step(i, _):
            j = jnp.clip(i - 2, 0, 7)
            results = []
            for w in range(2):
                result = []
                for t in range(3):
                    left = jnp.concatenate(
                        [vbuf[j, 64 * t : 64 * t + 64, 128 * w : 128 * w + 128], ones16], axis=0
                    )
                    result.append(nn(left, pbuf[w, :, 128 * t : 128 * t + 128]))
                results.append(result)
            where = pl.ds(pl.multiple_of(128 * j, 128), 128)
            for t in range(3):
                a, b = results[0][t], results[1][t]
                even = jnp.where(low, a[0:32], b[0:32])
                even = even * (1.0 / jnp.where(low, a[64:65], b[64:65]))
                odd = jnp.where(low, b[32:64], a[32:64])
                odd = odd * (1.0 / jnp.where(low, b[64:65], a[64:65]))
                mixbuf[32 * t : 32 * t + 32, where] = even.astype(BF16)
                mixbuf[96 + 32 * t : 128 + 32 * t, where] = odd.astype(BF16)

            for w in range(2):
                for t in range(3):
                    s = sbuf[w, :, 128 * t : 128 * t + 128] * (LOG2E * 32**-0.5)
                    s = s + biasl[ph, w, t]
                    s = s - jnp.max(s, axis=0, keepdims=True)
                    pbuf[w, :, 128 * t : 128 * t + 128] = jnp.exp2(s).astype(BF16)

            j = jnp.minimum(i, 7)
            for w in range(2):
                columns = []
                for t in range(3):
                    pieces = [zero64] * 3
                    pieces[t] = jnp.concatenate(
                        [
                            qbuf[j, w, 32 * t : 32 * t + 32],
                            qbuf[j, 1 - w, 96 + 32 * t : 128 + 32 * t],
                        ],
                        axis=0,
                    )
                    columns.append(jnp.concatenate(pieces, axis=0))
                start = pl.multiple_of(256 * j + 128 * w, 128)
                sbuf[w] = nn(kbuf[pl.ds(start, 128), :], jnp.concatenate(columns, axis=1))
            return 0

        lax.fori_loop(begin, end, step, 0, unroll=5)

    def mlp(ph):
        def first(j):
            cols = slice(256 * j, 256 * j + 256)
            prior_t = nt(eye(C), xbuf[ph, 4 * j : 4 * j + 4].reshape(256, C))
            odd = mixbuf[96:192, cols].astype(F32)
            odd = jnp.concatenate(
                [pltpu.roll(odd[:, 0:128], 64, 1), pltpu.roll(odd[:, 128:256], 64, 1)], axis=1
            ).astype(BF16)
            mixed = jnp.concatenate([mixbuf[0:96, cols], odd], axis=0)
            one = prior_t + nn(wout_t[...], mixed)
            onebuf[:, cols] = one
            mean = jnp.sum(one, axis=0, keepdims=True) * (1.0 / C)
            center = one - mean
            spread = jnp.sum(center * center, axis=0, keepdims=True) * (1.0 / C)
            nextbuf[:, cols] = (center * lax.rsqrt(spread + 1e-05)).astype(BF16)

        def second(j):
            cols = slice(256 * j, 256 * j + 256)
            actbuf[:, cols] = gelu(nn(wup_t[...], nextbuf[:, cols])).astype(BF16)

        def third(j):
            cols = slice(256 * j, 256 * j + 256)
            raised = nn(wdown[0], actbuf[0:384, cols]) + nn(wdown[1], actbuf[384:768, cols])
            two = (onebuf[:, cols] + raised).astype(BF16)
            fbuf[:, cols] = nn(head_t[...], two).astype(BF16)

        for j in range(6):
            if 0 <= j - 2 < 4:
                if ph == 0 and j == 2:
                    forwards[4].wait()
                third(j - 2)
            if 0 <= j - 1 < 4:
                second(j - 1)
            if j < 4:
                first(j)

    half_member = member // 2
    odd_member = lax.rem(member, 2)

    def send(ph):
        copies = []
        for k in (2, 1, 3, 0):
            pair = lax.rem(half_member + k, 4)
            cols = pl.ds(pl.multiple_of(256 * pair, 256), 256)
            sent = nn(fbuf[...], sendperm[:, cols]).astype(BF16)
            for j in range(2):
                sendbuf[ph, 2 * pair + j] = sent[:, 128 * j : 128 * j + 128]
            for j in range(2):
                to = 2 * pair + j
                if k == 0:
                    if j == 1:
                        continue
                    to = member + 1 - 2 * odd_member
                copy = pltpu.make_async_remote_copy(
                    src_ref=sendbuf.at[ph, to],
                    dst_ref=out.at[ph, member],
                    send_sem=a_send.at[ph, 2 * k + j],
                    recv_sem=a_recv.at[ph, 2 * k + odd_member],
                    device_id={"member": to},
                    device_id_type=MESH,
                )
                copy.start()
                copies.append(copy)
        mine = pltpu.make_async_copy(sendbuf.at[ph, member], out.at[ph, member], a_local.at[ph])
        mine.start()
        return copies, mine

    def finish(ph, copies, mine):
        for copy in copies:
            copy.wait_send()
        mine.wait()
        for k in (2, 1, 3, 0):
            for j in range(2):
                origin = 2 * lax.rem(half_member + 4 - k, 4) + j
                slot = 2 * k + j
                if k == 0:
                    if j == 1:
                        continue
                    origin = member + 1 - 2 * odd_member
                    slot = 1 - odd_member
                pltpu.make_async_remote_copy(
                    src_ref=sendbuf.at[ph, origin],
                    dst_ref=out.at[ph, origin],
                    send_sem=a_send.at[ph, slot],
                    recv_sem=a_recv.at[ph, slot],
                    device_id={"member": origin},
                    device_id_type=MESH,
                ).wait_recv()

    project(0)
    for i in range(2, 5):
        weights[i].wait()
        forwards[i].start()
    forwards[1].wait()

    key_i = iota((128, 128), 0)
    pos_i = iota((128, 128), 1)

    def position(index):
        return (
            jnp.bitwise_and(index // 8, 1) * 8 + jnp.bitwise_and(index // 16, 7)
        ) * 8 + jnp.bitwise_and(index, 7)

    natural = onehot(position(key_i) == pos_i)
    crossed = onehot(position(jnp.bitwise_xor(key_i, 64)) == pos_i)
    edge = jnp.logical_or(band == 0, band == BANDS - 1)
    straight = []
    swapped = []
    for h in range(6):
        turned = nt(natural, bias[h // 3, h % 3]).astype(BF16)
        straight.append(nt(turned, natural) * LOG2E)
        swapped.append(nt(turned, crossed) * LOG2E)
    for t in range(3):
        for w in range(2):
            lo, hi = (2 * t, 2 * t + 1) if w == 0 else (2 * t + 1, 2 * t)
            upper = jnp.where(low, straight[lo], swapped[hi])
            lower = jnp.where(low, swapped[lo], straight[hi])
            lower = jnp.concatenate([lower[64:128], lower[0:64]], axis=0)
            first_side = side[0] == 1
            biasl[0, w, t] = jnp.where(first_side, upper, lower)
            second = jnp.where(first_side, lower, upper)
            biasl[1, w, t] = jnp.where(jnp.logical_and(edge, key_i >= 64), -1e9, second)

    attend(0, 0, 10)
    forwards[2].wait()
    heads_in = [wout[h // 3, 32 * (h % 3) : 32 * (h % 3) + 32] for h in (0, 2, 4, 1, 3, 5)]
    wout_t[...] = nt(eye(C), jnp.concatenate(heads_in, axis=0)).astype(BF16)
    forwards[3].wait()
    for half in range(2):
        wup_t[half * 384 : half * 384 + 384, :] = nt(eye(384), wup[half]).astype(BF16)
    mlp(0)
    first_sent = send(0)
    halos[1].wait()
    halo_rows(1)
    project(1)
    attend(1, 0, 10)
    mlp(1)
    second_sent = send(1)
    finish(0, *first_sent)
    finish(1, *second_sent)


def forecast(off, prior, wqkv, wout, wup, wdown, bias, head):
    vmem = pltpu.VMEM
    dma = pltpu.SemaphoreType.DMA
    hbm = pl.BlockSpec(memory_space=pl.ANY)
    return pl.pallas_call(
        forecast_kernel,
        out_shape=jax.ShapeDtypeStruct((2, MEMBERS, NV, 128), BF16),
        in_specs=[pl.BlockSpec(memory_space=pltpu.SMEM)] + [hbm] * 7,
        out_specs=pl.BlockSpec(memory_space=pl.ANY),
        scratch_shapes=[
            vmem((2, 8, C, 128), BF16),
            vmem((2, 2, 4, C, 128), BF16),
            vmem((2, 3, C, 96), BF16),
            vmem((2, 96, C), BF16),
            vmem((2, C, 384), BF16),
            vmem((2, C, 384), BF16),
            vmem((2, 3, 128, 128), BF16),
            vmem((NV, C), BF16),
            vmem((3, C, C), BF16),
            vmem((C, C), BF16),
            vmem((FF, C), BF16),
            vmem((2, 2, 3, 128, 128), F32),
            vmem((256, 256), BF16),
            vmem((1024, 1024), BF16),
            vmem((2, 16, 8, 16, C), BF16),
            vmem((2, 16, 4, 16, C), BF16),
            vmem((2048, C), BF16),
            vmem((8, C, 256), BF16),
            vmem((8, 2, C, 128), BF16),
            vmem((2, 128, 384), F32),
            vmem((2, 128, 384), BF16),
            vmem((C, 1024), BF16),
            vmem((C, 1024), F32),
            vmem((C, 1024), BF16),
            vmem((FF, 1024), BF16),
            vmem((NV, 1024), BF16),
            vmem((2, MEMBERS, NV, 128), BF16),
            dma((7,)),
            dma((2,)),
            dma((2,)),
            dma((5,)),
            dma((5,)),
            dma((5,)),
            dma((5,)),
            dma((2, MEMBERS)),
            dma((2, MEMBERS)),
            dma((2,)),
        ],
        compiler_params=pltpu.CompilerParams(
            collective_id=0, has_side_effects=True, vmem_limit_bytes=60 * 1024 * 1024
        ),
        cost_estimate=pl.CostEstimate(
            flops=3_000_000_000, bytes_accessed=6_000_000, transcendentals=3_200_000
        ),
        name="forecast",
    )(off, prior, wqkv, wout, wup, wdown, bias, head)


def analysis_kernel(
    arrived,
    index_in,
    count_in,
    value_in,
    weight_in,
    out,
    recv,
    index,
    count,
    value,
    weight,
    in_sem,
    xf,
    vt,
    ybuf,
    obuf,
    work,
    scaled_ref,
    out_sem,
):
    parity = lax.rem(lax.axis_index("band"), 2)
    loads = []
    for ph in range(2):
        load = pltpu.make_async_copy(arrived.at[ph], recv.at[ph], in_sem.at[ph])
        load.start()
        loads.append(load)
    observations = []
    for n, (src, dst) in enumerate(
        ((index_in, index), (count_in, count), (value_in, value), (weight_in, weight))
    ):
        load = pltpu.make_async_copy(src, dst, in_sem.at[2 + n])
        load.start()
        observations.append(load)
    eye128 = eye(128)
    fold = onehot(jnp.bitwise_and(iota((64, 128), 1), 63) == iota((64, 128), 0))
    low_level = onehot(iota((1, 128), 1) < 64)
    high_level = onehot(iota((1, 128), 1) >= 64)
    for ph in range(2):
        base = 4 * (1 - parity) if ph == 0 else 4 * parity
        loads[ph].wait()
        for m in range(MEMBERS):
            block = recv[ph, m]
            both = jnp.concatenate([block * low_level, block * high_level], axis=0)
            xf[m, pl.ds(base * 16, 64), 0 : 2 * NV] = nt(fold, both)

    for load in observations:
        load.wait()
    lane = iota((128, 128), 1)
    pad = jnp.zeros((128, 112), jnp.int32)
    spread_index = jnp.concatenate([index[0].reshape(128, 16), pad], axis=1)
    idx = jnp.take_along_axis(spread_index, lane // 8, axis=1, mode="promise_in_bounds")
    tile = idx // 128
    inner = jnp.bitwise_and(idx, 127)
    slot_member = jnp.bitwise_and(lane, 7)
    observed = jnp.zeros((128, 128), F32)
    for m in range(MEMBERS):
        picks = []
        for part in range(3):
            x = xf[m, :, 128 * part : 128 * part + 128]
            picks.append(jnp.take_along_axis(x, inner, axis=1, mode="promise_in_bounds"))
        got = jnp.where(tile == 0, picks[0], jnp.where(tile == 1, picks[1], picks[2]))
        observed = jnp.where(slot_member == m, got, observed)
    obs_t = observed.T

    blank = jnp.zeros((128, 96), F32)
    terms = jnp.concatenate(
        [value[0].reshape(128, 16), weight[0].reshape(128, 16), blank], axis=1
    ).T
    counts = count[0].astype(F32).astype(BF16)
    spread = onehot(iota((16, 128), 0) == jnp.bitwise_and(iota((16, 128), 1), 15))
    wide = nn(counts, spread)
    live_count = jnp.sum(
        jnp.where(iota((8, 128), 0) == iota((8, 128), 1) // 16, wide, 0.0), axis=0, keepdims=True
    )

    sub = iota((8, 128), 0)
    rows = [jnp.zeros((8, 128), F32) for _ in range(MEMBERS)]
    right = jnp.zeros((8, 128), F32)
    devs = []
    for k in range(16):
        y = obs_t[8 * k : 8 * k + 8]
        mean = jnp.sum(y, axis=0, keepdims=True) * (1.0 / MEMBERS)
        dev = y - mean
        devs.append(dev)
        r = jnp.where(live_count > k, terms[16 + k : 17 + k], 0.0)
        scaled = dev * r
        right = right + scaled * (terms[k : k + 1] - mean)
        scaled_ref[k] = scaled
    for k in range(16):
        for i in range(MEMBERS):
            rows[i] = rows[i] + scaled_ref[k, i : i + 1, :] * devs[k]
    for i in range(MEMBERS):
        rows[i] = rows[i] + jnp.where(sub == i, MEMBERS - 1.0, 0.0)
    diagonal = jnp.zeros((8, 128), F32)
    for i in range(MEMBERS):
        diagonal = diagonal + jnp.where(sub == i, rows[i], 0.0)
    trace = jnp.sum(diagonal, axis=0, keepdims=True)
    inverse_trace = 1.0 / trace
    g = [row * inverse_trace for row in rows]

    def product(slot, right_mat):
        result = []
        for i in range(MEMBERS):
            terms_ = [work[slot, i, j : j + 1, :] * right_mat[j] for j in range(MEMBERS)]
            while len(terms_) > 1:
                terms_ = [terms_[n] + terms_[n + 1] for n in range(0, len(terms_), 2)]
            result.append(terms_[0])
        return result

    def keep(slot, mat):
        for i in range(MEMBERS):
            work[slot, i] = mat[i]

    def factor_of(zg):
        return [jnp.where(sub == i, 1.5, 0.0) - 0.5 * zg[i] for i in range(MEMBERS)]

    f = factor_of(g)
    keep(0, g)
    g = product(0, f)
    z = f
    keep(1, z)
    for step in range(1, NEWTON):
        f = factor_of(product(1, g))
        keep(2, f)
        if step < NEWTON - 1:
            keep(0, g)
            g = product(0, f)
        z = product(2, z)
        keep(1, z)

    def apply(mat, vec):
        total = mat[0] * vec[0:1]
        for j in range(1, MEMBERS):
            total = total + mat[j] * vec[j : j + 1]
        return total

    wbar = apply(z, apply(z, right)) * inverse_trace
    scale = math.sqrt(MEMBERS - 1.0) * lax.rsqrt(trace)
    full = [wbar[i : i + 1] + z[i] * scale for i in range(MEMBERS)]
    mean_row = full[0]
    for i in range(1, MEMBERS):
        mean_row = mean_row + full[i]
    shift = (1.0 - mean_row) * (1.0 / MEMBERS)
    low = iota((1, 128), 1) < 64
    for i in range(MEMBERS):
        value_i = full[i] + shift
        turned = pltpu.roll(value_i, 64, 1)
        first = jnp.where(low, value_i, turned)
        second = jnp.where(low, turned, value_i)
        vt[0, i] = jnp.where(parity == 1, first, second)
        vt[1, i] = jnp.where(parity == 1, second, first)

    def update(n, _):
        at = pl.ds(pl.multiple_of(n * 16, 16), 16)
        for ph in range(2):
            x = [recv[ph, i, at, :].astype(F32) for i in range(MEMBERS)]
            for m in range(MEMBERS):
                total = vt[ph, 0, m : m + 1, :] * x[0]
                for i in range(1, MEMBERS):
                    total = total + vt[ph, i, m : m + 1, :] * x[i]
                ybuf[ph, m, at, :] = total.astype(BF16)
        return 0

    lax.fori_loop(0, NV // 16, update, 0, unroll=True)

    copies = []
    for m in range(MEMBERS):
        for ph in range(2):
            base = 4 * (1 - parity) if ph == 0 else 4 * parity
            x = nt(eye128, ybuf[ph, m])
            obuf[m, :, pl.ds(base, 4), :, :] = x.reshape(2, 4, 16, NV)
        copy = pltpu.make_async_copy(obuf.at[m], out.at[m], out_sem.at[m])
        copy.start()
        copies.append(copy)
    for copy in copies:
        copy.wait()


def analyse(recv, index, count, value, weight):
    return pl.pallas_call(
        analysis_kernel,
        out_shape=jax.ShapeDtypeStruct((MEMBERS, 2, 8, 16, NV), F32),
        out_specs=pl.BlockSpec(memory_space=pl.ANY),
        in_specs=[pl.BlockSpec(memory_space=pl.ANY)] * 5,
        scratch_shapes=[
            pltpu.VMEM((2, MEMBERS, NV, 128), BF16),
            pltpu.VMEM((1, 8, 16, 16), jnp.int32),
            pltpu.VMEM((1, 8, 16), jnp.int32),
            pltpu.VMEM((1, 8, 16, 16), F32),
            pltpu.VMEM((1, 8, 16, 16), F32),
            pltpu.SemaphoreType.DMA((6,)),
            pltpu.VMEM((MEMBERS, 128, 384), F32),
            pltpu.VMEM((2, MEMBERS, MEMBERS, 128), F32),
            pltpu.VMEM((2, MEMBERS, NV, 128), BF16),
            pltpu.VMEM((MEMBERS, 2, 8, 16, NV), F32),
            pltpu.VMEM((3, MEMBERS, MEMBERS, 128), F32),
            pltpu.VMEM((16, MEMBERS, 128), F32),
            pltpu.SemaphoreType.DMA((MEMBERS,)),
        ],
        compiler_params=pltpu.CompilerParams(vmem_limit_bytes=60 * 1024 * 1024),
        cost_estimate=pl.CostEstimate(
            flops=20_000_000, bytes_accessed=3_000_000, transcendentals=0
        ),
        name="analyse",
    )(recv, index, count, value, weight)


def shards(
    prior_grids,
    w_qkv,
    w_out,
    w_up,
    w_down,
    head_weight,
    pos_bias,
    zonal_offsets,
    obs_index,
    obs_count,
    obs_value,
    obs_weight,
):
    recv = forecast(
        zonal_offsets,
        prior_grids.transpose(0, 1, 2, 4, 3),
        w_qkv.transpose(1, 0, 2),
        w_out,
        w_up,
        w_down.T,
        pos_bias,
        head_weight.T,
    )
    return analyse(recv, obs_index, obs_count, obs_value, obs_weight)


def solution(mesh):
    return jax.shard_map(
        shards,
        mesh=mesh,
        in_specs=(
            P("member", None, "band", None, None),
            P(None, None, "tensor"),
            P("tensor", None),
            P(None, "tensor"),
            P("tensor", None),
            P(),
            P("tensor", None, None),
            P("member"),
            P("tensor", "band", "member", None),
            P("tensor", "band", "member"),
            P("tensor", "band", "member", None),
            P("tensor", "band", "member", None),
        ),
        out_specs=P(None, "tensor", "band", "member", None),
        check_vma=False,
    )
```

```python
import functools
import math

import jax
import jax.numpy as jnp
from jax import lax
from jax.experimental import pallas as pl
from jax.experimental.pallas import tpu as pltpu
from jax.sharding import PartitionSpec as P

F32 = jnp.float32
BF16 = jnp.bfloat16
MESH = pl.DeviceIdType.MESH
C = 192
FF = 768
NV = 160
NEWTON = 8
MEMBERS = 8
BANDS = 16
LOG2E = 1.4426950408889634


def nt(a, b):
    return lax.dot_general(a, b, (((1,), (1,)), ((), ())), preferred_element_type=F32)


def nn(a, b):
    return jnp.dot(a, b, preferred_element_type=F32)


def iota(shape, dim):
    return lax.broadcasted_iota(jnp.int32, shape, dim)


def onehot(cond):
    return jnp.where(cond, 1.0, 0.0).astype(BF16)


def eye(n):
    return onehot(iota((n, n), 0) == iota((n, n), 1))


def gelu(x):
    return 0.5 * x * (1.0 + lax.erf(x * 0.7071067811865476))


def forecast_kernel(
    off_ref,
    prior,
    wqkv_in,
    wout_in,
    wup_in,
    wdown_in,
    bias_in,
    head_in,
    out,
    xown,
    halo,
    wqkv,
    wout,
    wup,
    wdown,
    bias,
    head_t,
    wqkv_t,
    wout_t,
    wup_t,
    biasl,
    perm,
    sendperm,
    nbuf,
    xbuf,
    kbuf,
    vbuf,
    qbuf,
    sbuf,
    pbuf,
    mixbuf,
    onebuf,
    nextbuf,
    actbuf,
    fbuf,
    sendbuf,
    local_sem,
    halo_send,
    halo_recv,
    w_send,
    w_recv,
    f_send,
    f_recv,
    a_send,
    a_recv,
    a_local,
):
    member = lax.axis_index("member")
    band = lax.axis_index("band")
    tensor = lax.axis_index("tensor")
    parity = lax.rem(band, 2)
    other = 1 - tensor
    sibling = band + 1 - 2 * parity
    far = lax.rem(band + 2 * parity - 1 + BANDS, BANDS)
    xband = lax.rem(band + BANDS // 2, BANDS)
    side = (1 - parity, parity)

    barrier = pltpu.get_barrier_semaphore()
    pl.semaphore_signal(barrier, inc=1, device_id={"band": sibling}, device_id_type=MESH)
    pl.semaphore_signal(barrier, inc=1, device_id={"band": far}, device_id_type=MESH)
    pl.semaphore_signal(
        barrier, inc=1, device_id={"band": xband, "tensor": other}, device_id_type=MESH
    )
    for k in range(1, MEMBERS):
        pl.semaphore_signal(
            barrier,
            inc=1,
            device_id={"member": lax.rem(member + k, MEMBERS)},
            device_id_type=MESH,
        )

    def part(ref, i, half, c):
        if i == 0:
            return ref.at[half, :, pl.ds(c * 96, 96)]
        if i == 1:
            return ref.at[half, :, pl.ds(c * 64, 64)]
        if i == 2:
            return ref.at[half, pl.ds(c * 48, 48)]
        return ref.at[half, pl.ds(c * 96, 96)]

    def src_part(ref, i, c):
        if i == 0:
            return ref.at[:, pl.ds(c * 96, 96)]
        if i == 1:
            return ref.at[:, pl.ds(c * 64, 64)]
        if i == 2:
            return ref.at[pl.ds(c * 48, 48)]
        return ref.at[pl.ds(c * 96, 96)]

    sources = (wqkv_in, bias_in, wout_in, wup_in, wdown_in)
    targets = (wqkv, bias, wout, wup, wdown)

    own_x = pltpu.make_async_copy(
        prior.at[0, pl.ds(2 * tensor, 2)], xown, local_sem.at[0]
    )
    own_x.start()
    locals_ = []
    for i in range(5):
        locals_.append(
            pltpu.make_async_copy(sources[i], targets[i].at[tensor], local_sem.at[1 + i])
        )
    locals_.append(pltpu.make_async_copy(head_in, head_t, local_sem.at[6]))
    for copy in locals_:
        copy.start()

    offset = off_ref[0]
    row_i = iota((256, 256), 0)
    col_i = iota((256, 256), 1)
    place = jnp.bitwise_and((row_i // 16) * 8 + jnp.bitwise_and(row_i, 7) + offset, 127)
    want = jnp.bitwise_and(row_i // 8, 1) * 128 + place
    perm[...] = onehot(want == col_i)

    def build_send(i, _):
        rows = iota((64, 1024), 0)
        cols = iota((64, 1024), 1)
        level = jnp.bitwise_and(rows // 8, 1)
        row = rows // 16
        where = jnp.bitwise_and(i * 8 + jnp.bitwise_and(rows, 7) + offset, 127)
        target = (where // 16) * 128 + level * 64 + row * 16 + jnp.bitwise_and(where, 15)
        sendperm[pl.ds(pl.multiple_of(i * 64, 64), 64), :] = onehot(target == cols)
        return 0

    pl.semaphore_wait(barrier, 3 + MEMBERS - 1)

    halos = []
    for ph, peer in ((0, sibling), (1, far)):
        halos.append(
            pltpu.make_async_remote_copy(
                src_ref=prior.at[0, pl.ds(2 * tensor, 2), pl.ds(4 * side[ph], 4)],
                dst_ref=halo.at[ph],
                send_sem=halo_send.at[ph],
                recv_sem=halo_recv.at[ph],
                device_id={"band": peer},
                device_id_type=MESH,
            )
        )
    weights = []
    forwards = []
    for i in range(5):
        weights.append(
            pltpu.make_async_remote_copy(
                src_ref=src_part(sources[i], i, parity),
                dst_ref=part(targets[i], i, tensor, parity),
                send_sem=w_send.at[i],
                recv_sem=w_recv.at[i],
                device_id={"band": xband, "tensor": other},
                device_id_type=MESH,
            )
        )
        piece = part(targets[i], i, other, parity)
        forwards.append(
            pltpu.make_async_remote_copy(
                src_ref=piece,
                dst_ref=piece,
                send_sem=f_send.at[i],
                recv_sem=f_recv.at[i],
                device_id={"band": sibling},
                device_id_type=MESH,
            )
        )
    weights[0].start()
    halos[0].start()
    weights[1].start()

    def prepare(block, ph, slot, keep):
        tokens = block.astype(F32)
        mean = jnp.sum(tokens, axis=0, keepdims=True) * (1.0 / C)
        center = tokens - mean
        spread = jnp.sum(center * center, axis=0, keepdims=True) * (1.0 / C)
        normed = (center * lax.rsqrt(spread + 1e-05)).astype(BF16)
        nbuf[ph, :, slot] = nt(perm[...], normed).astype(BF16).reshape(16, 16, C)
        if keep:
            xbuf[ph, :, slot] = nt(perm[...], block).astype(BF16).reshape(16, 16, C)

    own_x.wait()
    for ph in range(2):
        for r in range(4):
            row = 4 * side[ph] + r
            prepare(jnp.concatenate([xown[0, row], xown[1, row]], axis=1), ph, r, True)

    def halo_rows(ph):
        for r in range(4):
            prepare(jnp.concatenate([halo[ph, 0, r], halo[ph, 1, r]], axis=1), ph, 4 + r, False)

    for i in range(2, 5):
        weights[i].start()
    halos[1].start()
    lax.fori_loop(0, 16, build_send, 0)
    for copy in locals_:
        copy.wait()
    weights[0].wait()
    forwards[0].start()
    halos[0].wait()
    halo_rows(0)
    weights[1].wait()
    forwards[1].start()
    forwards[0].wait()

    for half in range(2):
        for i in range(3):
            turned = nt(eye(96), wqkv[half, i]).astype(BF16)
            if i > 0:
                wqkv_t[i, half * 96 : half * 96 + 96] = turned
                continue
            for n in range(3):
                h = 3 * half + n
                to = (h // 2) * 32 + (h % 2) * 96
                wqkv_t[0, to : to + 32] = turned[32 * n : 32 * n + 32]

    lane = iota((1, 128), 1)
    low = lane < 64

    def project(ph):
        wk, wv = wqkv_t[1], wqkv_t[2]
        wq_even, wq_odd = wqkv_t[0, 0:96], wqkv_t[0, 96:192]
        wide_low = jnp.bitwise_and(iota((1, 256), 1), 127) < 64
        for j in range(4):
            tokens = nbuf[ph, 4 * j : 4 * j + 4].reshape(512, C)
            own = nbuf[ph, 4 * j : 4 * j + 4, 0:4].reshape(4, 64, C)
            swapped = jnp.concatenate([own[1], own[0], own[3], own[2]], axis=0)
            kbuf[512 * j : 512 * j + 512, :] = nt(tokens, wk).astype(BF16)
            v = nt(wv, tokens).astype(BF16)
            q = jnp.concatenate([nt(wq_even, own.reshape(256, C)), nt(wq_odd, swapped)], axis=0)
            lows = jnp.where(wide_low, q, 0.0).astype(BF16)
            highs = jnp.where(wide_low, 0.0, q).astype(BF16)
            for i in range(2):
                vbuf[2 * j + i] = v[:, 256 * i : 256 * i + 256]
                qbuf[2 * j + i, 0] = lows[:, 128 * i : 128 * i + 128]
                qbuf[2 * j + i, 1] = highs[:, 128 * i : 128 * i + 128]

    zero64 = jnp.zeros((64, 128), BF16)
    ones16 = jnp.ones((16, 128), BF16)

    def attend(ph, begin, end):
        def combine(j):
            results = []
            for w in range(2):
                result = []
                for t in range(3):
                    left = jnp.concatenate(
                        [vbuf[j, 64 * t : 64 * t + 64, 128 * w : 128 * w + 128], ones16], axis=0
                    )
                    result.append(nn(left, pbuf[w, :, 128 * t : 128 * t + 128]))
                results.append(result)
            where = slice(128 * j, 128 * j + 128)
            for t in range(3):
                a, b = results[0][t], results[1][t]
                even = jnp.where(low, a[0:32], b[0:32])
                even = even * (1.0 / jnp.where(low, a[64:65], b[64:65]))
                odd = jnp.where(low, b[32:64], a[32:64])
                odd = odd * (1.0 / jnp.where(low, b[64:65], a[64:65]))
                mixbuf[32 * t : 32 * t + 32, where] = even.astype(BF16)
                mixbuf[96 + 32 * t : 128 + 32 * t, where] = odd.astype(BF16)

        def soften():
            for w in range(2):
                for t in range(3):
                    s = sbuf[w, :, 128 * t : 128 * t + 128] * (LOG2E * 32**-0.5)
                    s = s + biasl[ph, w, t]
                    s = s - jnp.max(s, axis=0, keepdims=True)
                    pbuf[w, :, 128 * t : 128 * t + 128] = jnp.exp2(s).astype(BF16)

        def score(j):
            for w in range(2):
                columns = []
                for t in range(3):
                    pieces = [zero64] * 3
                    pieces[t] = jnp.concatenate(
                        [
                            qbuf[j, w, 32 * t : 32 * t + 32],
                            qbuf[j, 1 - w, 96 + 32 * t : 128 + 32 * t],
                        ],
                        axis=0,
                    )
                    columns.append(jnp.concatenate(pieces, axis=0))
                start = 256 * j + 128 * w
                sbuf[w] = nn(kbuf[start : start + 128, :], jnp.concatenate(columns, axis=1))

        for i in range(begin, end):
            if i >= 2:
                combine(i - 2)
            if 1 <= i <= 8:
                soften()
            if i <= 7:
                score(i)

    def mlp(ph):
        def first(j):
            cols = slice(256 * j, 256 * j + 256)
            prior_t = nt(eye(C), xbuf[ph, 4 * j : 4 * j + 4].reshape(256, C))
            odd = mixbuf[96:192, cols].astype(F32)
            odd = jnp.concatenate(
                [pltpu.roll(odd[:, 0:128], 64, 1), pltpu.roll(odd[:, 128:256], 64, 1)], axis=1
            ).astype(BF16)
            mixed = jnp.concatenate([mixbuf[0:96, cols], odd], axis=0)
            one = prior_t + nn(wout_t[...], mixed)
            onebuf[:, cols] = one
            mean = jnp.sum(one, axis=0, keepdims=True) * (1.0 / C)
            center = one - mean
            spread = jnp.sum(center * center, axis=0, keepdims=True) * (1.0 / C)
            nextbuf[:, cols] = (center * lax.rsqrt(spread + 1e-05)).astype(BF16)

        def second(j):
            cols = slice(256 * j, 256 * j + 256)
            actbuf[:, cols] = gelu(nn(wup_t[...], nextbuf[:, cols])).astype(BF16)

        def third(j):
            cols = slice(256 * j, 256 * j + 256)
            raised = nn(wdown[0], actbuf[0:384, cols]) + nn(wdown[1], actbuf[384:768, cols])
            two = (onebuf[:, cols] + raised).astype(BF16)
            fbuf[:, cols] = nn(head_t[...], two).astype(BF16)

        for j in range(6):
            if 0 <= j - 2 < 4:
                if ph == 0 and j == 2:
                    forwards[4].wait()
                third(j - 2)
            if 0 <= j - 1 < 4:
                second(j - 1)
            if j < 4:
                first(j)

    half_member = member // 2
    odd_member = lax.rem(member, 2)

    def send(ph):
        copies = []
        for k in (2, 1, 3, 0):
            pair = lax.rem(half_member + k, 4)
            cols = pl.ds(pl.multiple_of(256 * pair, 256), 256)
            sent = nn(fbuf[...], sendperm[:, cols]).astype(BF16)
            for j in range(2):
                sendbuf[ph, 2 * pair + j] = sent[:, 128 * j : 128 * j + 128]
            for j in range(2):
                to = 2 * pair + j
                if k == 0:
                    if j == 1:
                        continue
                    to = member + 1 - 2 * odd_member
                copy = pltpu.make_async_remote_copy(
                    src_ref=sendbuf.at[ph, to],
                    dst_ref=out.at[ph, member],
                    send_sem=a_send.at[ph, 2 * k + j],
                    recv_sem=a_recv.at[ph, 2 * k + odd_member],
                    device_id={"member": to},
                    device_id_type=MESH,
                )
                copy.start()
                copies.append(copy)
        mine = pltpu.make_async_copy(sendbuf.at[ph, member], out.at[ph, member], a_local.at[ph])
        mine.start()
        return copies, mine

    def finish(ph, copies, mine):
        for copy in copies:
            copy.wait_send()
        mine.wait()
        for k in (2, 1, 3, 0):
            for j in range(2):
                origin = 2 * lax.rem(half_member + 4 - k, 4) + j
                slot = 2 * k + j
                if k == 0:
                    if j == 1:
                        continue
                    origin = member + 1 - 2 * odd_member
                    slot = 1 - odd_member
                pltpu.make_async_remote_copy(
                    src_ref=sendbuf.at[ph, origin],
                    dst_ref=out.at[ph, origin],
                    send_sem=a_send.at[ph, slot],
                    recv_sem=a_recv.at[ph, slot],
                    device_id={"member": origin},
                    device_id_type=MESH,
                ).wait_recv()

    project(0)
    for i in range(2, 5):
        weights[i].wait()
        forwards[i].start()
    forwards[1].wait()

    key_i = iota((128, 128), 0)
    pos_i = iota((128, 128), 1)

    def position(index):
        return (
            jnp.bitwise_and(index // 8, 1) * 8 + jnp.bitwise_and(index // 16, 7)
        ) * 8 + jnp.bitwise_and(index, 7)

    natural = onehot(position(key_i) == pos_i)
    crossed = onehot(position(jnp.bitwise_xor(key_i, 64)) == pos_i)
    edge = jnp.logical_or(band == 0, band == BANDS - 1)
    straight = []
    swapped = []
    for h in range(6):
        turned = nt(natural, bias[h // 3, h % 3]).astype(BF16)
        straight.append(nt(turned, natural) * LOG2E)
        swapped.append(nt(turned, crossed) * LOG2E)
    for t in range(3):
        for w in range(2):
            lo, hi = (2 * t, 2 * t + 1) if w == 0 else (2 * t + 1, 2 * t)
            upper = jnp.where(low, straight[lo], swapped[hi])
            lower = jnp.where(low, swapped[lo], straight[hi])
            lower = jnp.concatenate([lower[64:128], lower[0:64]], axis=0)
            first_side = side[0] == 1
            biasl[0, w, t] = jnp.where(first_side, upper, lower)
            second = jnp.where(first_side, lower, upper)
            biasl[1, w, t] = jnp.where(jnp.logical_and(edge, key_i >= 64), -1e9, second)

    attend(0, 0, 10)
    forwards[2].wait()
    heads_in = [wout[h // 3, 32 * (h % 3) : 32 * (h % 3) + 32] for h in (0, 2, 4, 1, 3, 5)]
    wout_t[...] = nt(eye(C), jnp.concatenate(heads_in, axis=0)).astype(BF16)
    forwards[3].wait()
    for half in range(2):
        wup_t[half * 384 : half * 384 + 384, :] = nt(eye(384), wup[half]).astype(BF16)
    mlp(0)
    first_sent = send(0)
    halos[1].wait()
    halo_rows(1)
    project(1)
    attend(1, 0, 10)
    mlp(1)
    second_sent = send(1)
    finish(0, *first_sent)
    finish(1, *second_sent)


def forecast(off, prior, wqkv, wout, wup, wdown, bias, head):
    vmem = pltpu.VMEM
    dma = pltpu.SemaphoreType.DMA
    hbm = pl.BlockSpec(memory_space=pl.ANY)
    return pl.pallas_call(
        forecast_kernel,
        out_shape=jax.ShapeDtypeStruct((2, MEMBERS, NV, 128), BF16),
        in_specs=[pl.BlockSpec(memory_space=pltpu.SMEM)] + [hbm] * 7,
        out_specs=pl.BlockSpec(memory_space=pl.ANY),
        scratch_shapes=[
            vmem((2, 8, C, 128), BF16),
            vmem((2, 2, 4, C, 128), BF16),
            vmem((2, 3, C, 96), BF16),
            vmem((2, 96, C), BF16),
            vmem((2, C, 384), BF16),
            vmem((2, C, 384), BF16),
            vmem((2, 3, 128, 128), BF16),
            vmem((NV, C), BF16),
            vmem((3, C, C), BF16),
            vmem((C, C), BF16),
            vmem((FF, C), BF16),
            vmem((2, 2, 3, 128, 128), F32),
            vmem((256, 256), BF16),
            vmem((1024, 1024), BF16),
            vmem((2, 16, 8, 16, C), BF16),
            vmem((2, 16, 4, 16, C), BF16),
            vmem((2048, C), BF16),
            vmem((8, C, 256), BF16),
            vmem((8, 2, C, 128), BF16),
            vmem((2, 128, 384), F32),
            vmem((2, 128, 384), BF16),
            vmem((C, 1024), BF16),
            vmem((C, 1024), F32),
            vmem((C, 1024), BF16),
            vmem((FF, 1024), BF16),
            vmem((NV, 1024), BF16),
            vmem((2, MEMBERS, NV, 128), BF16),
            dma((7,)),
            dma((2,)),
            dma((2,)),
            dma((5,)),
            dma((5,)),
            dma((5,)),
            dma((5,)),
            dma((2, MEMBERS)),
            dma((2, MEMBERS)),
            dma((2,)),
        ],
        compiler_params=pltpu.CompilerParams(
            collective_id=0, has_side_effects=True, vmem_limit_bytes=60 * 1024 * 1024
        ),
        cost_estimate=pl.CostEstimate(
            flops=3_000_000_000, bytes_accessed=6_000_000, transcendentals=3_200_000
        ),
        name="forecast",
    )(off, prior, wqkv, wout, wup, wdown, bias, head)


def analysis_kernel(
    arrived,
    index_in,
    count_in,
    value_in,
    weight_in,
    out,
    recv,
    index,
    count,
    value,
    weight,
    in_sem,
    xf,
    vt,
    ybuf,
    obuf,
    work,
    scaled_ref,
    out_sem,
):
    parity = lax.rem(lax.axis_index("band"), 2)
    loads = []
    for ph in range(2):
        load = pltpu.make_async_copy(arrived.at[ph], recv.at[ph], in_sem.at[ph])
        load.start()
        loads.append(load)
    observations = []
    for n, (src, dst) in enumerate(
        ((index_in, index), (count_in, count), (value_in, value), (weight_in, weight))
    ):
        load = pltpu.make_async_copy(src, dst, in_sem.at[2 + n])
        load.start()
        observations.append(load)
    eye128 = eye(128)
    fold = onehot(jnp.bitwise_and(iota((64, 128), 1), 63) == iota((64, 128), 0))
    low_level = onehot(iota((1, 128), 1) < 64)
    high_level = onehot(iota((1, 128), 1) >= 64)
    for ph in range(2):
        base = 4 * (1 - parity) if ph == 0 else 4 * parity
        loads[ph].wait()
        for m in range(MEMBERS):
            block = recv[ph, m]
            both = jnp.concatenate([block * low_level, block * high_level], axis=0)
            xf[m, pl.ds(base * 16, 64), 0 : 2 * NV] = nt(fold, both)

    for load in observations:
        load.wait()
    lane = iota((128, 128), 1)
    pad = jnp.zeros((128, 112), jnp.int32)
    spread_index = jnp.concatenate([index[0].reshape(128, 16), pad], axis=1)
    idx = jnp.take_along_axis(spread_index, lane // 8, axis=1, mode="promise_in_bounds")
    tile = idx // 128
    inner = jnp.bitwise_and(idx, 127)
    slot_member = jnp.bitwise_and(lane, 7)
    observed = jnp.zeros((128, 128), F32)
    for m in range(MEMBERS):
        picks = []
        for part in range(3):
            x = xf[m, :, 128 * part : 128 * part + 128]
            picks.append(jnp.take_along_axis(x, inner, axis=1, mode="promise_in_bounds"))
        got = jnp.where(tile == 0, picks[0], jnp.where(tile == 1, picks[1], picks[2]))
        observed = jnp.where(slot_member == m, got, observed)
    obs_t = observed.T

    blank = jnp.zeros((128, 96), F32)
    terms = jnp.concatenate(
        [value[0].reshape(128, 16), weight[0].reshape(128, 16), blank], axis=1
    ).T
    counts = count[0].astype(F32).astype(BF16)
    spread = onehot(iota((16, 128), 0) == jnp.bitwise_and(iota((16, 128), 1), 15))
    wide = nn(counts, spread)
    live_count = jnp.sum(
        jnp.where(iota((8, 128), 0) == iota((8, 128), 1) // 16, wide, 0.0), axis=0, keepdims=True
    )

    sub = iota((8, 128), 0)
    rows = [jnp.zeros((8, 128), F32) for _ in range(MEMBERS)]
    right = jnp.zeros((8, 128), F32)
    devs = []
    for k in range(16):
        y = obs_t[8 * k : 8 * k + 8]
        mean = jnp.sum(y, axis=0, keepdims=True) * (1.0 / MEMBERS)
        dev = y - mean
        devs.append(dev)
        r = jnp.where(live_count > k, terms[16 + k : 17 + k], 0.0)
        scaled = dev * r
        right = right + scaled * (terms[k : k + 1] - mean)
        scaled_ref[k] = scaled
    for k in range(16):
        for i in range(MEMBERS):
            rows[i] = rows[i] + scaled_ref[k, i : i + 1, :] * devs[k]
    for i in range(MEMBERS):
        rows[i] = rows[i] + jnp.where(sub == i, MEMBERS - 1.0, 0.0)
    diagonal = jnp.zeros((8, 128), F32)
    for i in range(MEMBERS):
        diagonal = diagonal + jnp.where(sub == i, rows[i], 0.0)
    trace = jnp.sum(diagonal, axis=0, keepdims=True)
    inverse_trace = 1.0 / trace
    g = [row * inverse_trace for row in rows]

    def product(slot, right_mat):
        result = []
        for i in range(MEMBERS):
            terms_ = [work[slot, i, j : j + 1, :] * right_mat[j] for j in range(MEMBERS)]
            while len(terms_) > 1:
                terms_ = [terms_[n] + terms_[n + 1] for n in range(0, len(terms_), 2)]
            result.append(terms_[0])
        return result

    def keep(slot, mat):
        for i in range(MEMBERS):
            work[slot, i] = mat[i]

    def factor_of(zg):
        return [jnp.where(sub == i, 1.5, 0.0) - 0.5 * zg[i] for i in range(MEMBERS)]

    f = factor_of(g)
    keep(0, g)
    g = product(0, f)
    z = f
    keep(1, z)
    for step in range(1, NEWTON):
        f = factor_of(product(1, g))
        keep(2, f)
        if step < NEWTON - 1:
            keep(0, g)
            g = product(0, f)
        z = product(2, z)
        keep(1, z)

    def apply(mat, vec):
        total = mat[0] * vec[0:1]
        for j in range(1, MEMBERS):
            total = total + mat[j] * vec[j : j + 1]
        return total

    wbar = apply(z, apply(z, right)) * inverse_trace
    scale = math.sqrt(MEMBERS - 1.0) * lax.rsqrt(trace)
    full = [wbar[i : i + 1] + z[i] * scale for i in range(MEMBERS)]
    mean_row = full[0]
    for i in range(1, MEMBERS):
        mean_row = mean_row + full[i]
    shift = (1.0 - mean_row) * (1.0 / MEMBERS)
    low = iota((1, 128), 1) < 64
    for i in range(MEMBERS):
        value_i = full[i] + shift
        turned = pltpu.roll(value_i, 64, 1)
        first = jnp.where(low, value_i, turned)
        second = jnp.where(low, turned, value_i)
        vt[0, i] = jnp.where(parity == 1, first, second)
        vt[1, i] = jnp.where(parity == 1, second, first)

    def update(n, _):
        at = pl.ds(pl.multiple_of(n * 16, 16), 16)
        for ph in range(2):
            x = [recv[ph, i, at, :].astype(F32) for i in range(MEMBERS)]
            for m in range(MEMBERS):
                total = vt[ph, 0, m : m + 1, :] * x[0]
                for i in range(1, MEMBERS):
                    total = total + vt[ph, i, m : m + 1, :] * x[i]
                ybuf[ph, m, at, :] = total.astype(BF16)
        return 0

    lax.fori_loop(0, NV // 16, update, 0, unroll=True)

    copies = []
    for m in range(MEMBERS):
        for ph in range(2):
            base = 4 * (1 - parity) if ph == 0 else 4 * parity
            x = nt(eye128, ybuf[ph, m])
            obuf[m, :, pl.ds(base, 4), :, :] = x.reshape(2, 4, 16, NV)
        copy = pltpu.make_async_copy(obuf.at[m], out.at[m], out_sem.at[m])
        copy.start()
        copies.append(copy)
    for copy in copies:
        copy.wait()


def analyse(recv, index, count, value, weight):
    return pl.pallas_call(
        analysis_kernel,
        out_shape=jax.ShapeDtypeStruct((MEMBERS, 2, 8, 16, NV), F32),
        out_specs=pl.BlockSpec(memory_space=pl.ANY),
        in_specs=[pl.BlockSpec(memory_space=pl.ANY)] * 5,
        scratch_shapes=[
            pltpu.VMEM((2, MEMBERS, NV, 128), BF16),
            pltpu.VMEM((1, 8, 16, 16), jnp.int32),
            pltpu.VMEM((1, 8, 16), jnp.int32),
            pltpu.VMEM((1, 8, 16, 16), F32),
            pltpu.VMEM((1, 8, 16, 16), F32),
            pltpu.SemaphoreType.DMA((6,)),
            pltpu.VMEM((MEMBERS, 128, 384), F32),
            pltpu.VMEM((2, MEMBERS, MEMBERS, 128), F32),
            pltpu.VMEM((2, MEMBERS, NV, 128), BF16),
            pltpu.VMEM((MEMBERS, 2, 8, 16, NV), F32),
            pltpu.VMEM((3, MEMBERS, MEMBERS, 128), F32),
            pltpu.VMEM((16, MEMBERS, 128), F32),
            pltpu.SemaphoreType.DMA((MEMBERS,)),
        ],
        compiler_params=pltpu.CompilerParams(vmem_limit_bytes=60 * 1024 * 1024),
        cost_estimate=pl.CostEstimate(
            flops=20_000_000, bytes_accessed=3_000_000, transcendentals=0
        ),
        name="analyse",
    )(recv, index, count, value, weight)


def shards(
    prior_grids,
    w_qkv,
    w_out,
    w_up,
    w_down,
    head_weight,
    pos_bias,
    zonal_offsets,
    obs_index,
    obs_count,
    obs_value,
    obs_weight,
):
    recv = forecast(
        zonal_offsets,
        prior_grids.transpose(0, 1, 2, 4, 3),
        w_qkv.transpose(1, 0, 2),
        w_out,
        w_up,
        w_down.T,
        pos_bias,
        head_weight.T,
    )
    return analyse(recv, obs_index, obs_count, obs_value, obs_weight)


def solution(mesh):
    return jax.shard_map(
        shards,
        mesh=mesh,
        in_specs=(
            P("member", None, "band", None, None),
            P(None, None, "tensor"),
            P("tensor", None),
            P(None, "tensor"),
            P("tensor", None),
            P(),
            P("tensor", None, None),
            P("member"),
            P("tensor", "band", "member", None),
            P("tensor", "band", "member"),
            P("tensor", "band", "member", None),
            P("tensor", "band", "member", None),
        ),
        out_specs=P(None, "tensor", "band", "member", None),
        check_vma=False,
    )
```
